512 devices in a mesh: depth: 8 (over y), lat: 32 (over z, x), freq: 2 (over core).
Axes of the slice: x: 4, y: 8, z: 8, core: 2. Of those that a mesh axis runs over, the one named last changes fastest.
Arguments:
- surface: bfloat16 [6, 2, 128, 32768], P('freq', None, None, 'lat'), may hold values from -6 to 6
- refl: float32 [8, 32768], P('depth', 'lat'), may hold values from -0.5 to 0.5
- pool: bfloat16 [8, 6, 8, 128, 256], P('depth', 'freq'), may hold values from -0.375 to 0.375
- tile_ids: int32 [8, 256, 10], P('depth', 'lat'), may hold values from 0 to 255, as said below
- block_ids: int32 [8, 256, 10], P('depth', 'lat'), may hold values from 0 to 7
- counts: int32 [8, 256], P('depth', 'lat'), may hold values from 1 to 10, as said below
Outputs:
- image: float32 [8, 32768], P('depth', 'lat')
The draws below stay inside these ranges and needn't reach their ends.
Inputs may be any that keep to these rules, and one draw needn't show every extreme that they name: tile_ids[l, j, k] = (j + o) mod 256 for an offset o with -8 <= o <= 8; slot 0 names the row's own tile; in every level some row has all 10 slots live with offsets 8 at slot 1 and -8 at slot 2. Slots k >= counts[l, j] of row j are padding; in every level some row has all 10 slots live.
All inputs are finite; a program needn't handle non-finite values.
Results may differ from the reference program's by a relative error of at most 0.00055.
Values may be sent and summed in bfloat16 or wider, within the bound.
A program may use at most 128 MiB of HBM per device.

```python
import jax
import jax.numpy as jnp
from jax import lax

TILE = 128
SLOTS = 10
POOL = 8
TILE_DEV = 8
SHOTS = 128
LEVELS = 8
FREQS = 6
TILES = 256
NX = 32768
APER = 8


def aperture_lists(key):
    offset_key = jax.random.fold_in(key, 11)
    row_key = jax.random.fold_in(key, 12)
    heavy_key = jax.random.fold_in(key, 13)
    base_key = jax.random.fold_in(key, 14)
    extra_key = jax.random.fold_in(key, 15)
    offsets = jax.random.randint(offset_key, (LEVELS, TILES, SLOTS), -APER, APER + 1)
    slot_index = jnp.arange(SLOTS)[None, None, :]
    row_index = jnp.arange(TILES)[None, :, None]
    chosen_row = jax.random.randint(row_key, (LEVELS,), 0, TILES)
    is_chosen = jnp.arange(TILES)[None, :] == chosen_row[:, None]
    offsets = jnp.where(slot_index == 0, 0, offsets)
    offsets = jnp.where(is_chosen[:, :, None] & (slot_index == 1), APER, offsets)
    offsets = jnp.where(is_chosen[:, :, None] & (slot_index == 2), -APER, offsets)
    tile_lists = jnp.mod(row_index + offsets, TILES).astype(jnp.int32)
    heavy_region = (jax.random.randint(heavy_key, (LEVELS, TILES // TILE_DEV), 0, 4) == 0).astype(jnp.int32)
    heavy_rows = jnp.repeat(heavy_region, TILE_DEV, axis=1)
    base_count = 3 + jax.random.randint(base_key, (LEVELS, TILES), 0, 3)
    extra_count = jax.random.randint(extra_key, (LEVELS, TILES), 0, SLOTS - 4)
    live_counts = jnp.where(is_chosen, SLOTS, base_count + heavy_rows * extra_count).astype(jnp.int32)
    return (tile_lists, live_counts)


def draw_tile_ids(key, part):
    return aperture_lists(key)[0]


def draw_counts(key, part):
    return aperture_lists(key)[1]


def plant(array, key, least, high):
    spot = [jax.random.randint(jax.random.fold_in(key, axis), (), 0, length) for axis, length in enumerate(array.shape)]
    main_axis = array.shape.index(max(array.shape))
    neighbour = spot[:main_axis] + [(spot[main_axis] + 1) % array.shape[main_axis]] + spot[main_axis + 1:]
    return array.at[tuple(spot)].set(least).at[tuple(neighbour)].set(high)


def shard_levels(key, dims, shards, smallest, largest):
    factor_of = 1.0
    for position, parts in shards:
        draws = jax.random.uniform(jax.random.fold_in(jax.random.fold_in(key, 6), position), (parts,), jnp.float32, smallest / len(shards), largest / len(shards))
        factor_of = factor_of * jnp.repeat(jnp.exp(draws), dims[position] // parts).reshape((-1,) + (1,) * (len(dims) - 1 - position))
    return factor_of


def normal_values(own_key, extent, deviation, reach, cuts=(), kind=jnp.bfloat16):
    level = shard_levels(own_key, extent, cuts, -0.22, 0.18) if cuts else 1.0
    drawn = jax.random.normal(own_key, extent, jnp.float32) * deviation * level
    return jnp.minimum(jnp.maximum(drawn, -reach), reach).astype(kind)


def setup_inputs(seed: int = 0) -> dict:
    streams_of = jax.random.split(jax.random.key(seed), 7)
    surface = normal_values(streams_of[0], (FREQS, 2, SHOTS, NX), 1.0, 6.0, ((0, 2), (3, 32)))
    refl = jnp.clip(jax.random.uniform(streams_of[1], (LEVELS, NX), jnp.float32, -0.5, 0.5) * shard_levels(streams_of[1], (LEVELS, NX), ((0, 8), (1, 32)), -0.4, 0.0), -0.5, 0.5)
    pool = normal_values(streams_of[2], (LEVELS, FREQS, POOL, TILE, 2 * TILE), (2 * TILE) ** -0.5, 0.375, ((0, 8), (1, 2)))
    tile_ids = draw_tile_ids(jax.random.fold_in(streams_of[6], 71), 0)
    block_ids = plant(jax.random.randint(streams_of[4], (LEVELS, TILES, SLOTS), 0, POOL), jax.random.fold_in(streams_of[4], 1), 0, POOL - 1).astype(jnp.int32)
    counts = draw_counts(jax.random.fold_in(streams_of[6], 71), 0)
    return dict(surface=surface, refl=refl, pool=pool, tile_ids=tile_ids, block_ids=block_ids, counts=counts)


def advance(wave_field, pool_level, ids_level, blocks_level, counts_level, refl_level):
    tile_grid = wave_field.reshape(FREQS, 2, SHOTS, TILES, TILE)
    slot_index = jnp.arange(SLOTS, dtype=jnp.int32)

    def one_row(row_args):
        row_ids, row_blocks, row_count = row_args
        slot_live = (slot_index < row_count).astype(jnp.float32)
        picked = jnp.take(tile_grid, row_ids.astype(jnp.int32), axis=3).astype(jnp.float32)
        picked = picked * slot_live[None, None, None, :, None]
        chosen = jnp.take(pool_level, row_blocks.astype(jnp.int32), axis=1).astype(jnp.float32)
        product = jnp.einsum('fsakt,fktc->fsac', picked, chosen)
        real_part = product[:, 0, :, :TILE] - product[:, 1, :, TILE:]
        imag_part = product[:, 0, :, TILE:] + product[:, 1, :, :TILE]
        row_scale = 1.0 / jnp.sqrt(row_count.astype(jnp.float32))
        return jnp.stack([real_part, imag_part], 1) * row_scale
    rows_out = lax.map(one_row, (ids_level, blocks_level, counts_level))
    wave_out = jnp.transpose(rows_out, (1, 2, 3, 0, 4)).reshape(FREQS, 2, SHOTS, NX)
    wave_out = wave_out * (1.0 - refl_level)
    level_image = lax.optimization_barrier(jnp.sum(wave_out * wave_out, axis=(0, 1, 2))) / (FREQS * SHOTS)
    return (wave_out.astype(jnp.bfloat16), level_image)

def reference(surface, refl, pool, tile_ids, block_ids, counts):
    wave_field = surface
    images = []
    for level_index in range(LEVELS):
        wave_field, level_image = advance(wave_field, pool[level_index], tile_ids[level_index], block_ids[level_index], counts[level_index], refl[level_index])
        images.append(level_image)
    return jnp.stack(images, 0)
```

```python
import jax
import jax.numpy as jnp
from jax import lax
from jax.experimental import pallas as pl
from jax.experimental.pallas import tpu as pltpu
from jax.sharding import PartitionSpec as P

MESH = pl.DeviceIdType.MESH
ANY = pl.BlockSpec(memory_space=pl.ANY)
BF = jnp.bfloat16
F32 = jnp.float32
DEAD = 8 * 1024


def place():
    d = lax.axis_index("depth")
    a = lax.axis_index("lat")
    c = lax.axis_index("freq")
    return d, a // 4, a % 4, c


def remote(src, dst, send, recv, d, z, x, c):
    return pltpu.make_async_remote_copy(
        src_ref=src,
        dst_ref=dst,
        send_sem=send,
        recv_sem=recv,
        device_id=(d, z * 4 + x, c),
        device_id_type=MESH,
    )


def spread_kernel(
    wsrc, fac, ints, pool, wave, fac_all, ints_all, pool_all,
    w_send, w_recv, y_send, y_recv, x_send, x_recv, z_send, z_recv, s_send, s_recv,
    p_send, p_recv, q_send, q_recv, l_sem,
):
    d, z, x, c = place()
    a = z * 4 + x
    other = 1 - c
    active = z < 6
    own_core = z // 3
    half = pl.ds(4 * c, 4)

    mine = pool.at[0, z % 3]
    here = pltpu.make_async_copy(mine, pool_all.at[d], l_sem.at[0])
    over = remote(mine, pool_all.at[d], q_send.at[7], q_recv.at[7], d, z, x, other)
    gives = jnp.logical_and(active, c == own_core)
    takes = jnp.logical_and(active, c != own_core)

    @pl.when(gives)
    def _():
        over.start()
        here.start()

    near = d // 4 == c
    fac_here = pltpu.make_async_copy(fac, fac_all.at[d, z, x], l_sem.at[1])
    ints_here = pltpu.make_async_copy(ints, ints_all.at[d, z, x], l_sem.at[2])

    def y_copies(step):
        to = (d + step) % 8
        return (
            remote(fac, fac_all.at[d, z, x], y_send.at[0, step], y_recv.at[0, d % 4], to, z, x, c),
            remote(ints, ints_all.at[d, z, x], y_send.at[1, step], y_recv.at[1, d % 4], to, z, x, c),
        )

    @pl.when(near)
    def _():
        fac_here.start()
        ints_here.start()
        for step in range(1, 8):
            for copy in y_copies(step):
                copy.start()

    def w_copy(i):
        part, u = i // 8, i % 8
        return (
            wsrc.at[part, u], 3 * c + part, u // 2, u % 2
        )

    def w_self(tz, tx, tc):
        return jnp.logical_and(tz * 4 + tx == a, tc == c)

    @pl.loop(0, 24)
    def _(i):
        src, tz, tx, tc = w_copy(i)
        same = w_self(tz, tx, tc)

        @pl.when(same)
        def _():
            pltpu.make_async_copy(src, wave.at[a], l_sem.at[3]).start()

        @pl.when(jnp.logical_not(same))
        def _():
            remote(src, wave.at[a], w_send.at[i], w_recv.at[a], d, tz, tx, tc).start()

    @pl.when(near)
    def _():
        fac_here.wait()
        ints_here.wait()

    for k in range(4):
        level = 4 * c + k

        @pl.when(level != d)
        def _():
            for kind, whole in ((0, fac_all), (1, ints_all)):
                pltpu.make_async_copy(
                    whole.at[level, z, x], whole.at[level, z, x], y_recv.at[kind, k]
                ).wait()

    def x_copies(step):
        to = (x + step) % 4
        return [
            remote(whole.at[half, z, x], whole.at[half, z, x], x_send.at[kind, step],
                   x_recv.at[kind, step], d, z, to, c)
            for kind, whole in ((0, fac_all), (1, ints_all))
        ]

    for step in range(1, 4):
        for copy in x_copies(step):
            copy.start()

    @pl.when(gives)
    def _():
        here.wait()

    @pl.when(takes)
    def _():
        over.wait_recv()

    def ring_copy(way, step):
        if way == 0:
            level, to = (d - step + 8) % 8, (d + 1) % 8
        else:
            level, to = (d + step) % 8, (d + 7) % 8
        at = pool_all.at[level, half]
        return remote(at, at, p_send.at[way, step], p_recv.at[way, step], to, z, x, c)

    def share(way, step):
        level = (d - 1 - step + 8) % 8 if way == 0 else (d + 1 + step) % 8
        at = pool_all.at[level, half]
        i = step if way == 0 else 4 + step
        return remote(at, at, q_send.at[i], q_recv.at[i], d, z, x, other)

    @pl.when(active)
    def _():
        ring_copy(0, 0).start()
        ring_copy(1, 0).start()

    for step in range(1, 4):
        for copy in x_copies(step):
            copy.wait_recv()

    def z_copies(step):
        to = (z + step) % 8
        return to, [
            remote(whole.at[half, z], whole.at[half, z], z_send.at[kind, step],
                   z_recv.at[kind, step], d, to, x, c)
            for kind, whole in ((0, fac_all), (1, ints_all))
        ]

    for step in range(1, 8):
        to, copies = z_copies(step)

        @pl.when(to < 6)
        def _():
            for copy in copies:
                copy.start()

    @pl.when(active)
    def _():
        for step in range(4):
            ring_copy(0, step).wait_recv()
            if step < 3:
                ring_copy(0, step + 1).start()
            share(0, step).start()
            if step < 3:
                ring_copy(1, step).wait_recv()
                if step < 2:
                    ring_copy(1, step + 1).start()
                share(1, step).start()

        for step in range(1, 8):
            for copy in z_copies(step)[1]:
                copy.wait_recv()
        swaps = [
            remote(whole.at[half], whole.at[half], s_send.at[kind], s_recv.at[kind], d, z, x, other)
            for kind, whole in ((0, fac_all), (1, ints_all))
        ]
        for copy in swaps:
            copy.start()
        for copy in swaps:
            copy.wait()
        for way, step in ((0, 0), (0, 1), (0, 2), (0, 3), (1, 0), (1, 1), (1, 2)):
            ring_copy(way, step).wait_send()
            share(way, step).wait()

        @pl.loop(0, 32)
        def _(i):
            same = jnp.logical_and(i == a, c == own_core)

            @pl.when(same)
            def _():
                pltpu.make_async_copy(wave.at[i], wave.at[i], l_sem.at[3]).wait()

            @pl.when(jnp.logical_not(same))
            def _():
                pltpu.make_async_copy(wave.at[i], wave.at[i], w_recv.at[i]).wait()

    @pl.when(gives)
    def _():
        over.wait_send()

    @pl.when(near)
    def _():
        for step in range(1, 8):
            for copy in y_copies(step):
                copy.wait_send()

    for step in range(1, 4):
        for copy in x_copies(step):
            copy.wait_send()
    for step in range(1, 8):
        to, copies = z_copies(step)

        @pl.when(to < 6)
        def _():
            for copy in copies:
                copy.wait_send()

    @pl.loop(0, 24)
    def _(i):
        src, tz, tx, tc = w_copy(i)

        @pl.when(jnp.logical_not(w_self(tz, tx, tc)))
        def _():
            remote(src, wave.at[a], w_send.at[i], w_recv.at[a], d, tz, tx, tc).wait_send()


def spread(wsrc, fac, ints, pool):
    dma = pltpu.SemaphoreType.DMA
    return pl.pallas_call(
        spread_kernel,
        out_shape=(
            jax.ShapeDtypeStruct((32, 32, 128), BF),
            jax.ShapeDtypeStruct((8, 8, 4, 8, 128), F32),
            jax.ShapeDtypeStruct((8, 8, 4, 1, 128), jnp.int32),
            jax.ShapeDtypeStruct((8, 8, 128, 256), BF),
        ),
        in_specs=[ANY] * 4,
        out_specs=(ANY,) * 4,
        scratch_shapes=[
            dma((24,)), dma((32,)),
            dma((2, 8)), dma((2, 4)), dma((2, 4)), dma((2, 4)), dma((2, 8)), dma((2, 8)),
            dma((2,)), dma((2,)),
            dma((2, 4)), dma((2, 4)), dma((8,)), dma((8,)), dma((4,)),
        ],
        compiler_params=pltpu.CompilerParams(has_side_effects=True),
        name="spread",
    )(wsrc, fac, ints, pool)


def levels_kernel(ints, wave, fac, pool, image, field, prod, rows):
    level = pl.program_id(0)
    _, z, _, _ = place()

    @pl.when(z < 6)
    def _():
        @pl.when(level == 0)
        def _():
            prod[DEAD : DEAD + 8, :] = jnp.zeros((8, 128), F32)

            @pl.loop(0, 16)
            def _(i):
                pair = [wave[2 * i + k].astype(F32) for k in range(2)]
                at = pl.ds(pl.multiple_of(16 * i, 16), 16)
                put_field(
                    field, at,
                    [jnp.concatenate([p[8 * q : 8 * q + 8] for p in pair], 0) for q in range(4)],
                )

        for pair in range(4):
            b0, b1 = pool[0, 2 * pair], pool[0, 2 * pair + 1]
            weights = jnp.concatenate(
                [
                    jnp.concatenate([b0[:, :128], b1[:, :128]], 1),
                    jnp.concatenate([b0[:, 128:], b1[:, 128:]], 1),
                ],
                0,
            )
            for q in range(4):
                out = jnp.dot(field[q], weights, preferred_element_type=F32)
                for k in range(2):
                    base = (2 * pair + k) * 1024 + q
                    prod[pl.ds(base, 256, stride=4), :] = out[:, 128 * k : 128 * k + 128]

        @pl.loop(0, 32)
        def _(g):
            most = ints[level, g, 80]

            def slot(k, sums):
                return tuple(
                    sums[r] + prod[pl.ds(ints[level, g, k * 8 + r], 4), :] for r in range(8)
                )

            sums = lax.fori_loop(0, most, slot, tuple(jnp.zeros((4, 128), F32) for _ in range(8)))
            for r in range(8):
                rows[pl.ds(pl.multiple_of(g * 32, 32) + 4 * r, 4), :] = sums[r]

        @pl.loop(0, 16)
        def _(i):
            at = pl.ds(pl.multiple_of(16 * i, 16), 16)
            scale = fac[0, at, :]
            new = [rows[pl.ds(64 * i + q, 16, stride=4), :] * scale for q in range(4)]
            image[0, at, :] = (new[0] * new[0] + new[1] * new[1]) + (
                new[2] * new[2] + new[3] * new[3]
            )
            put_field(field, at, new)


def put_field(field, at, parts):
    for s in range(2):
        re, im = parts[2 * s].astype(BF), parts[2 * s + 1].astype(BF)
        field[2 * s, at, :128] = re
        field[2 * s, at, 128:] = -im
        field[2 * s + 1, at, :128] = im
        field[2 * s + 1, at, 128:] = re


def levels(ints, wave, fac, pool):
    return pl.pallas_call(
        levels_kernel,
        grid=(8,),
        out_shape=jax.ShapeDtypeStruct((8, 256, 128), F32),
        in_specs=[
            pl.BlockSpec(memory_space=pltpu.SMEM),
            pl.BlockSpec((32, 32, 128), lambda i: (0, 0, 0)),
            pl.BlockSpec((1, 256, 128), lambda i: (i, 0, 0)),
            pl.BlockSpec((1, 8, 128, 256), lambda i: (i, 0, 0, 0)),
        ],
        out_specs=pl.BlockSpec((1, 256, 128), lambda i: (i, 0, 0)),
        scratch_shapes=[
            pltpu.VMEM((4, 256, 256), BF),
            pltpu.VMEM((DEAD + 8, 128), F32),
            pltpu.VMEM((1024, 128), F32),
        ],
        compiler_params=pltpu.CompilerParams(vmem_limit_bytes=40 * 2**20),
        name="levels",
    )(ints, wave, fac, pool)


def collect_kernel(
    part, out, got, in_sib, half_sum, in_x, x_sum, in_y, y_sum, in_z, done,
    l_sem, s_send, s_recv, x_send, x_recv, y_send, y_recv, z_send, z_recv, e_send, e_recv,
):
    d, z, x, c = place()
    other = 1 - c
    active = z < 6
    near = d // 4 == c
    half = pl.ds(4 * c, 4)

    @pl.when(active)
    def _():
        give = remote(part.at[pl.ds(4 * other, 4)], in_sib, s_send.at[0], s_recv.at[0], d, z, x, other)
        give.start()
        keep = pltpu.make_async_copy(part.at[half], half_sum, l_sem.at[0])
        keep.start()
        keep.wait()
        give.wait()

        @pl.loop(0, 4)
        def _(k):
            half_sum[k] = half_sum[k] + in_sib[k]

        def x_copy(step):
            to = (x + step) % 4
            return remote(half_sum.at[:, :, to], in_x.at[step], x_send.at[step], x_recv.at[step], d, z, to, c)

        for step in range(1, 4):
            x_copy(step).start()
        for step in range(1, 4):
            x_copy(step).wait_recv()
        @pl.loop(0, 4)
        def _(k):
            x_sum[k] = (half_sum[k, :, x] + in_x[1, k]) + (in_x[2, k] + in_x[3, k])

        def y_copy(k):
            return remote(x_sum.at[k], in_y.at[d], y_send.at[k], y_recv.at[d], 4 * c + k, z, x, c)

        for k in range(4):
            @pl.when(4 * c + k != d)
            def _():
                y_copy(k).start()

        @pl.when(near)
        def _():
            for s in range(8):
                @pl.when(d != s)
                def _():
                    pltpu.make_async_copy(in_y.at[s], in_y.at[s], y_recv.at[s]).wait()
            total = x_sum[d % 4]
            for step in range(1, 8):
                total = total + in_y[(d + step) % 8]
            y_sum[...] = total

            for step in range(1, 8):
                to = (z + step) % 8
                remote(y_sum.at[to], in_z.at[z], z_send.at[step], z_recv.at[z], d, to, x, c).start()

        for k in range(4):
            @pl.when(4 * c + k != d)
            def _():
                y_copy(k).wait_send()
        for step in range(1, 4):
            x_copy(step).wait_send()

    echo = remote(done, got, e_send.at[0], e_recv.at[0], d, z, x, other)

    @pl.when(near)
    def _():
        @pl.when(active)
        def _():
            in_z[z] = y_sum[z]

        for s in range(6):
            @pl.when(z != s)
            def _():
                pltpu.make_async_copy(in_z.at[s], in_z.at[s], z_recv.at[s]).wait()
        total = in_z[0]
        for s in range(1, 6):
            total = total + in_z[s]
        done[...] = total / 768.0
        echo.start()
        out[...] = done[...]

        @pl.when(active)
        def _():
            for step in range(1, 8):
                to = (z + step) % 8
                remote(y_sum.at[to], in_z.at[z], z_send.at[step], z_recv.at[z], d, to, x, c).wait_send()
        echo.wait_send()

    @pl.when(jnp.logical_not(near))
    def _():
        echo.wait_recv()
        out[...] = got[...]


def collect(part):
    dma = pltpu.SemaphoreType.DMA
    vmem = lambda *shape: pltpu.VMEM(shape, F32)
    return pl.pallas_call(
        collect_kernel,
        out_shape=jax.ShapeDtypeStruct((8, 128), F32),
        in_specs=[ANY],
        out_specs=pl.BlockSpec(memory_space=pltpu.VMEM),
        scratch_shapes=[
            vmem(8, 128),
            vmem(4, 8, 4, 8, 128), vmem(4, 8, 4, 8, 128),
            vmem(4, 4, 8, 8, 128), vmem(4, 8, 8, 128),
            vmem(8, 8, 8, 128), vmem(8, 8, 128),
            vmem(8, 8, 128), vmem(8, 128),
            dma((1,)), dma((1,)), dma((1,)), dma((4,)), dma((4,)), dma((4,)), dma((8,)),
            dma((8,)), dma((8,)), dma((1,)), dma((1,)),
        ],
        compiler_params=pltpu.CompilerParams(
            has_side_effects=True, vmem_limit_bytes=24 * 2**20
        ),
        name="collect",
    )(part)


def per_device(surface, refl, pool, tile_ids, block_ids, counts):
    d = lax.axis_index("depth")
    own = lax.dynamic_slice_in_dim(surface, d * 16, 16, 2)
    own = own.reshape(3, 2, 8, 2, 8, 128)
    wsrc = jnp.transpose(own, (0, 2, 3, 1, 4, 5)).reshape(3, 8, 32, 128)
    scale = 1.0 / jnp.sqrt(counts[0].astype(F32))
    fac = (1.0 - refl.reshape(8, 128)) * scale[:, None]
    live = jnp.arange(10)[None, :] < counts[0][:, None]
    slots = jnp.where(live, block_ids[0] * 1024 + tile_ids[0] * 4, DEAD)
    ints = jnp.concatenate(
        [slots.T.reshape(1, 80), jnp.max(counts).reshape(1, 1), jnp.zeros((1, 47), jnp.int32)], 1
    ).astype(jnp.int32)
    wave, fac_all, ints_all, pool_all = spread(wsrc, fac, ints, pool)
    part = levels(
        ints_all.reshape(8, 32, 128), wave, fac_all.reshape(8, 256, 128), pool_all
    )
    return collect(part.reshape(8, 8, 4, 8, 128)).reshape(1, 1024)


def solution(mesh):
    placed = (
        P("freq", None, None, "lat"),
        P("depth", "lat"),
        P("depth", "freq", None, None, None),
        P("depth", "lat", None),
        P("depth", "lat", None),
        P("depth", "lat"),
    )
    return jax.shard_map(
        per_device, mesh=mesh, in_specs=placed, out_specs=P("depth", "lat"), check_vma=False
    )
```

```python
import jax
import jax.numpy as jnp
from jax import lax
from jax.experimental import pallas as pl
from jax.experimental.pallas import tpu as pltpu
from jax.sharding import PartitionSpec as P

MESH = pl.DeviceIdType.MESH
ANY = pl.BlockSpec(memory_space=pl.ANY)
BF = jnp.bfloat16
F32 = jnp.float32
DEAD = 8 * 1024


def place():
    d = lax.axis_index("depth")
    a = lax.axis_index("lat")
    c = lax.axis_index("freq")
    return d, a // 4, a % 4, c


def remote(src, dst, send, recv, d, z, x, c):
    return pltpu.make_async_remote_copy(
        src_ref=src,
        dst_ref=dst,
        send_sem=send,
        recv_sem=recv,
        device_id=(d, z * 4 + x, c),
        device_id_type=MESH,
    )


def greet(peers):
    barrier = pltpu.get_barrier_semaphore()
    for d, z, x, c in peers:
        pl.semaphore_signal(barrier, inc=1, device_id=(d, z * 4 + x, c), device_id_type=MESH)
    pl.semaphore_wait(barrier, len(peers))


def spread_kernel(
    wsrc, fac, ints, pool, wave, fac_all, ints_all, pool_all,
    w_send, w_recv, y_send, y_recv, x_send, x_recv, z_send, z_recv, s_send, s_recv,
    p_send, p_recv, q_send, q_recv, l_sem,
):
    d, z, x, c = place()
    a = z * 4 + x
    other = 1 - c
    active = z < 6
    own_core = z // 3
    half = pl.ds(4 * c, 4)

    greet(
        [(d, (z + i) % 8, (x + j) % 4, c) for i in range(8) for j in range(4) if i or j]
        + [(d, (z + i) % 8, (x + j) % 4, other) for i in range(8) for j in range(4)]
        + [((d + i) % 8, z, x, c) for i in range(1, 8)]
    )

    mine = pool.at[0, z % 3]
    here = pltpu.make_async_copy(mine, pool_all.at[d], l_sem.at[0])
    over = remote(mine, pool_all.at[d], q_send.at[7], q_recv.at[7], d, z, x, other)
    gives = jnp.logical_and(active, c == own_core)
    takes = jnp.logical_and(active, c != own_core)

    @pl.when(gives)
    def _():
        over.start()
        here.start()

    near = d // 4 == c
    fac_here = pltpu.make_async_copy(fac, fac_all.at[d, z, x], l_sem.at[1])
    ints_here = pltpu.make_async_copy(ints, ints_all.at[d, z, x], l_sem.at[2])

    def y_copies(step):
        to = (d + step) % 8
        return (
            remote(fac, fac_all.at[d, z, x], y_send.at[0, step], y_recv.at[0, d % 4], to, z, x, c),
            remote(ints, ints_all.at[d, z, x], y_send.at[1, step], y_recv.at[1, d % 4], to, z, x, c),
        )

    @pl.when(near)
    def _():
        fac_here.start()
        ints_here.start()
        for step in range(1, 8):
            for copy in y_copies(step):
                copy.start()

    def w_copy(i):
        part, u = i // 8, i % 8
        return (
            wsrc.at[part, u], 3 * c + part, u // 2, u % 2
        )

    def w_self(tz, tx, tc):
        return jnp.logical_and(tz * 4 + tx == a, tc == c)

    @pl.loop(0, 24)
    def _(i):
        src, tz, tx, tc = w_copy(i)
        same = w_self(tz, tx, tc)

        @pl.when(same)
        def _():
            pltpu.make_async_copy(src, wave.at[a], l_sem.at[3]).start()

        @pl.when(jnp.logical_not(same))
        def _():
            remote(src, wave.at[a], w_send.at[i], w_recv.at[a], d, tz, tx, tc).start()

    @pl.when(near)
    def _():
        fac_here.wait()
        ints_here.wait()

    for k in range(4):
        level = 4 * c + k

        @pl.when(level != d)
        def _():
            for kind, whole in ((0, fac_all), (1, ints_all)):
                pltpu.make_async_copy(
                    whole.at[level, z, x], whole.at[level, z, x], y_recv.at[kind, k]
                ).wait()

    def x_copies(step):
        to = (x + step) % 4
        return [
            remote(whole.at[half, z, x], whole.at[half, z, x], x_send.at[kind, step],
                   x_recv.at[kind, step], d, z, to, c)
            for kind, whole in ((0, fac_all), (1, ints_all))
        ]

    for step in range(1, 4):
        for copy in x_copies(step):
            copy.start()

    @pl.when(gives)
    def _():
        here.wait()

    @pl.when(takes)
    def _():
        over.wait_recv()

    def ring_copy(way, step):
        if way == 0:
            level, to = (d - step + 8) % 8, (d + 1) % 8
        else:
            level, to = (d + step) % 8, (d + 7) % 8
        at = pool_all.at[level, half]
        return remote(at, at, p_send.at[way, step], p_recv.at[way, step], to, z, x, c)

    def share(way, step):
        level = (d - 1 - step + 8) % 8 if way == 0 else (d + 1 + step) % 8
        at = pool_all.at[level, half]
        i = step if way == 0 else 4 + step
        return remote(at, at, q_send.at[i], q_recv.at[i], d, z, x, other)

    @pl.when(active)
    def _():
        ring_copy(0, 0).start()
        ring_copy(1, 0).start()

    for step in range(1, 4):
        for copy in x_copies(step):
            copy.wait_recv()

    def z_copies(step):
        to = (z + step) % 8
        return to, [
            remote(whole.at[half, z], whole.at[half, z], z_send.at[kind, step],
                   z_recv.at[kind, step], d, to, x, c)
            for kind, whole in ((0, fac_all), (1, ints_all))
        ]

    for step in range(1, 8):
        to, copies = z_copies(step)

        @pl.when(to < 6)
        def _():
            for copy in copies:
                copy.start()

    @pl.when(active)
    def _():
        for step in range(4):
            ring_copy(0, step).wait_recv()
            if step < 3:
                ring_copy(0, step + 1).start()
            share(0, step).start()
            if step < 3:
                ring_copy(1, step).wait_recv()
                if step < 2:
                    ring_copy(1, step + 1).start()
                share(1, step).start()

        for step in range(1, 8):
            for copy in z_copies(step)[1]:
                copy.wait_recv()
        swaps = [
            remote(whole.at[half], whole.at[half], s_send.at[kind], s_recv.at[kind], d, z, x, other)
            for kind, whole in ((0, fac_all), (1, ints_all))
        ]
        for copy in swaps:
            copy.start()
        for copy in swaps:
            copy.wait()
        for way, step in ((0, 0), (0, 1), (0, 2), (0, 3), (1, 0), (1, 1), (1, 2)):
            ring_copy(way, step).wait_send()
            share(way, step).wait()

        @pl.loop(0, 32)
        def _(i):
            same = jnp.logical_and(i == a, c == own_core)

            @pl.when(same)
            def _():
                pltpu.make_async_copy(wave.at[i], wave.at[i], l_sem.at[3]).wait()

            @pl.when(jnp.logical_not(same))
            def _():
                pltpu.make_async_copy(wave.at[i], wave.at[i], w_recv.at[i]).wait()

    @pl.when(gives)
    def _():
        over.wait_send()

    @pl.when(near)
    def _():
        for step in range(1, 8):
            for copy in y_copies(step):
                copy.wait_send()

    for step in range(1, 4):
        for copy in x_copies(step):
            copy.wait_send()
    for step in range(1, 8):
        to, copies = z_copies(step)

        @pl.when(to < 6)
        def _():
            for copy in copies:
                copy.wait_send()

    @pl.loop(0, 24)
    def _(i):
        src, tz, tx, tc = w_copy(i)

        @pl.when(jnp.logical_not(w_self(tz, tx, tc)))
        def _():
            remote(src, wave.at[a], w_send.at[i], w_recv.at[a], d, tz, tx, tc).wait_send()


def spread(wsrc, fac, ints, pool):
    dma = pltpu.SemaphoreType.DMA
    return pl.pallas_call(
        spread_kernel,
        out_shape=(
            jax.ShapeDtypeStruct((32, 32, 128), BF),
            jax.ShapeDtypeStruct((8, 8, 4, 8, 128), F32),
            jax.ShapeDtypeStruct((8, 8, 4, 1, 128), jnp.int32),
            jax.ShapeDtypeStruct((8, 8, 128, 256), BF),
        ),
        in_specs=[ANY] * 4,
        out_specs=(ANY,) * 4,
        scratch_shapes=[
            dma((24,)), dma((32,)),
            dma((2, 8)), dma((2, 4)), dma((2, 4)), dma((2, 4)), dma((2, 8)), dma((2, 8)),
            dma((2,)), dma((2,)),
            dma((2, 4)), dma((2, 4)), dma((8,)), dma((8,)), dma((4,)),
        ],
        compiler_params=pltpu.CompilerParams(has_side_effects=True, collective_id=1),
        name="spread",
    )(wsrc, fac, ints, pool)


def levels_kernel(ints, wave, fac, pool, image, field, prod, rows):
    level = pl.program_id(0)
    _, z, _, _ = place()

    @pl.when(z < 6)
    def _():
        @pl.when(level == 0)
        def _():
            prod[DEAD : DEAD + 8, :] = jnp.zeros((8, 128), F32)

            @pl.loop(0, 16)
            def _(i):
                pair = [wave[2 * i + k].astype(F32) for k in range(2)]
                at = pl.ds(pl.multiple_of(16 * i, 16), 16)
                put_field(
                    field, at,
                    [jnp.concatenate([p[8 * q : 8 * q + 8] for p in pair], 0) for q in range(4)],
                )

        for pair in range(4):
            b0, b1 = pool[0, 2 * pair], pool[0, 2 * pair + 1]
            weights = jnp.concatenate(
                [
                    jnp.concatenate([b0[:, :128], b1[:, :128]], 1),
                    jnp.concatenate([b0[:, 128:], b1[:, 128:]], 1),
                ],
                0,
            )
            for q in range(4):
                out = jnp.dot(field[q], weights, preferred_element_type=F32)
                for k in range(2):
                    base = (2 * pair + k) * 1024 + q
                    prod[pl.ds(base, 256, stride=4), :] = out[:, 128 * k : 128 * k + 128]

        @pl.loop(0, 16)
        def _(g):
            most = jnp.maximum(ints[level, 2 * g, 80], ints[level, 2 * g + 1, 80])

            def add(slots):
                for r in range(16):
                    at = [ints[level, 2 * g + r // 8, k * 8 + r % 8] for k in range(slots)]
                    parts = [prod[pl.ds(i, 4), :] for i in at]
                    while len(parts) > 1:
                        parts = [sum(parts[i : i + 2]) for i in range(0, len(parts), 2)]
                    rows[pl.ds(pl.multiple_of(g * 64, 64) + 4 * r, 4), :] = parts[0]

            @pl.when(most <= 5)
            def _():
                add(5)

            @pl.when(most > 5)
            def _():
                add(10)

        @pl.loop(0, 16)
        def _(i):
            at = pl.ds(pl.multiple_of(16 * i, 16), 16)
            scale = fac[0, at, :]
            new = [rows[pl.ds(64 * i + q, 16, stride=4), :] * scale for q in range(4)]
            image[0, at, :] = (new[0] * new[0] + new[1] * new[1]) + (
                new[2] * new[2] + new[3] * new[3]
            )
            put_field(field, at, new)


def put_field(field, at, parts):
    for s in range(2):
        re, im = parts[2 * s].astype(BF), parts[2 * s + 1].astype(BF)
        field[2 * s, at, :128] = re
        field[2 * s, at, 128:] = -im
        field[2 * s + 1, at, :128] = im
        field[2 * s + 1, at, 128:] = re


def levels(ints, wave, fac, pool):
    return pl.pallas_call(
        levels_kernel,
        grid=(8,),
        out_shape=jax.ShapeDtypeStruct((8, 256, 128), F32),
        in_specs=[
            pl.BlockSpec(memory_space=pltpu.SMEM),
            pl.BlockSpec((32, 32, 128), lambda i: (0, 0, 0)),
            pl.BlockSpec((1, 256, 128), lambda i: (i, 0, 0)),
            pl.BlockSpec((1, 8, 128, 256), lambda i: (i, 0, 0, 0)),
        ],
        out_specs=pl.BlockSpec((1, 256, 128), lambda i: (i, 0, 0)),
        scratch_shapes=[
            pltpu.VMEM((4, 256, 256), BF),
            pltpu.VMEM((DEAD + 8, 128), F32),
            pltpu.VMEM((1024, 128), F32),
        ],
        compiler_params=pltpu.CompilerParams(vmem_limit_bytes=60 * 2**20),
        name="levels",
    )(ints, wave, fac, pool)


def collect_kernel(
    part, out, got, in_sib, half_sum, in_x, x_sum, in_y, y_sum, in_z, done,
    l_sem, s_send, s_recv, x_send, x_recv, y_send, y_recv, z_send, z_recv, e_send, e_recv,
):
    d, z, x, c = place()
    other = 1 - c
    active = z < 6
    near = d // 4 == c
    half = pl.ds(4 * c, 4)

    greet(
        [(d, z, x, other)]
        + [(d, z, (x + i) % 4, c) for i in range(1, 4)]
        + [(d, (z + i) % 8, x, c) for i in range(1, 8)]
        + [((d + i) % 8, z, x, c) for i in range(1, 8)]
    )

    @pl.when(active)
    def _():
        give = remote(part.at[pl.ds(4 * other, 4)], in_sib, s_send.at[0], s_recv.at[0], d, z, x, other)
        give.start()
        keep = pltpu.make_async_copy(part.at[half], half_sum, l_sem.at[0])
        keep.start()
        keep.wait()
        give.wait()

        @pl.loop(0, 4)
        def _(k):
            half_sum[k] = half_sum[k] + in_sib[k]

        def x_copy(step):
            to = (x + step) % 4
            return remote(half_sum.at[:, :, to], in_x.at[step], x_send.at[step], x_recv.at[step], d, z, to, c)

        for step in range(1, 4):
            x_copy(step).start()
        for step in range(1, 4):
            x_copy(step).wait_recv()
        @pl.loop(0, 4)
        def _(k):
            x_sum[k] = (half_sum[k, :, x] + in_x[1, k]) + (in_x[2, k] + in_x[3, k])

        def y_copy(k):
            return remote(x_sum.at[k], in_y.at[d], y_send.at[k], y_recv.at[d], 4 * c + k, z, x, c)

        for k in range(4):
            @pl.when(4 * c + k != d)
            def _():
                y_copy(k).start()

        @pl.when(near)
        def _():
            for s in range(8):
                @pl.when(d != s)
                def _():
                    pltpu.make_async_copy(in_y.at[s], in_y.at[s], y_recv.at[s]).wait()
            total = x_sum[d % 4]
            for step in range(1, 8):
                total = total + in_y[(d + step) % 8]
            y_sum[...] = total

            for step in range(1, 8):
                to = (z + step) % 8
                remote(y_sum.at[to], in_z.at[z], z_send.at[step], z_recv.at[z], d, to, x, c).start()

        for k in range(4):
            @pl.when(4 * c + k != d)
            def _():
                y_copy(k).wait_send()
        for step in range(1, 4):
            x_copy(step).wait_send()

    echo = remote(done, got, e_send.at[0], e_recv.at[0], d, z, x, other)

    @pl.when(near)
    def _():
        @pl.when(active)
        def _():
            in_z[z] = y_sum[z]

        for s in range(6):
            @pl.when(z != s)
            def _():
                pltpu.make_async_copy(in_z.at[s], in_z.at[s], z_recv.at[s]).wait()
        total = in_z[0]
        for s in range(1, 6):
            total = total + in_z[s]
        done[...] = total / 768.0
        echo.start()
        out[...] = done[...]

        @pl.when(active)
        def _():
            for step in range(1, 8):
                to = (z + step) % 8
                remote(y_sum.at[to], in_z.at[z], z_send.at[step], z_recv.at[z], d, to, x, c).wait_send()
        echo.wait_send()

    @pl.when(jnp.logical_not(near))
    def _():
        echo.wait_recv()
        out[...] = got[...]


def collect(part):
    dma = pltpu.SemaphoreType.DMA
    vmem = lambda *shape: pltpu.VMEM(shape, F32)
    return pl.pallas_call(
        collect_kernel,
        out_shape=jax.ShapeDtypeStruct((8, 128), F32),
        in_specs=[ANY],
        out_specs=pl.BlockSpec(memory_space=pltpu.VMEM),
        scratch_shapes=[
            vmem(8, 128),
            vmem(4, 8, 4, 8, 128), vmem(4, 8, 4, 8, 128),
            vmem(4, 4, 8, 8, 128), vmem(4, 8, 8, 128),
            vmem(8, 8, 8, 128), vmem(8, 8, 128),
            vmem(8, 8, 128), vmem(8, 128),
            dma((1,)), dma((1,)), dma((1,)), dma((4,)), dma((4,)), dma((4,)), dma((8,)),
            dma((8,)), dma((8,)), dma((1,)), dma((1,)),
        ],
        compiler_params=pltpu.CompilerParams(
            has_side_effects=True, vmem_limit_bytes=60 * 2**20, collective_id=2
        ),
        name="collect",
    )(part)


def per_device(surface, refl, pool, tile_ids, block_ids, counts):
    d = lax.axis_index("depth")
    own = lax.dynamic_slice_in_dim(surface, d * 16, 16, 2)
    own = own.reshape(3, 2, 8, 2, 8, 128)
    wsrc = jnp.transpose(own, (0, 2, 3, 1, 4, 5)).reshape(3, 8, 32, 128)
    scale = 1.0 / jnp.sqrt(counts[0].astype(F32))
    fac = (1.0 - refl.reshape(8, 128)) * scale[:, None]
    live = jnp.arange(10)[None, :] < counts[0][:, None]
    slots = jnp.where(live, block_ids[0] * 1024 + tile_ids[0] * 4, DEAD)
    ints = jnp.concatenate(
        [slots.T.reshape(1, 80), jnp.max(counts).reshape(1, 1), jnp.zeros((1, 47), jnp.int32)], 1
    ).astype(jnp.int32)
    wave, fac_all, ints_all, pool_all = spread(wsrc, fac, ints, pool)
    part = levels(
        ints_all.reshape(8, 32, 128), wave, fac_all.reshape(8, 256, 128), pool_all
    )
    return collect(part.reshape(8, 8, 4, 8, 128)).reshape(1, 1024)


def solution(mesh):
    placed = (
        P("freq", None, None, "lat"),
        P("depth", "lat"),
        P("depth", "freq", None, None, None),
        P("depth", "lat", None),
        P("depth", "lat", None),
        P("depth", "lat"),
    )
    return jax.shard_map(
        per_device, mesh=mesh, in_specs=placed, out_specs=P("depth", "lat"), check_vma=False
    )
```

```python
import jax
import jax.numpy as jnp
from jax import lax
from jax.experimental import pallas as pl
from jax.experimental.pallas import tpu as pltpu
from jax.sharding import PartitionSpec as P

MESH = pl.DeviceIdType.MESH
ANY = pl.BlockSpec(memory_space=pl.ANY)
VMEM = pl.BlockSpec(memory_space=pltpu.VMEM)
BF = jnp.bfloat16
F32 = jnp.float32
WIDE = 144
DEAD = 8 * WIDE


def remote(src, dst, send, recv, d, z, x, c):
    return pltpu.make_async_remote_copy(
        src_ref=src,
        dst_ref=dst,
        send_sem=send,
        recv_sem=recv,
        device_id=(d, z * 4 + x, c),
        device_id_type=MESH,
    )


def arrival(ref, sem):
    return pltpu.make_async_copy(ref, ref, sem)


def turned(rows):
    count = rows.shape[0]
    even = lax.broadcasted_iota(jnp.int32, rows.shape, 0) % 2 == 0
    return jnp.where(even, -pltpu.roll(rows, count - 1, 0), pltpu.roll(rows, 1, 0))


def kernel(
    wsrc, fac, ints, pool, out,
    wave, field, pool_all, fac_all, ints_all, lists, prod, img, in_x, x_sum, in_yz, done, got,
    l_sem, w_send, w_recv, y_send, y_recv, z_send, z_recv, x_send, x_recv,
    p_send, p_recv, q_send, q_recv, h_send, h_recv, i_send, i_recv, o_send, o_recv, e_sem,
):
    d = lax.axis_index("depth")
    a = lax.axis_index("lat")
    c = lax.axis_index("freq")
    z, x = a // 4, a % 4
    other = 1 - c
    active = z < 6
    side = z // 4
    near = side == c
    source = z // 3
    gives = jnp.logical_and(active, c == source)
    takes = jnp.logical_and(active, c != source)
    half = pl.ds(4 * c, 4)

    def wave_out(i):
        return 3 * c + i // 4, i % 4, side

    def wave_in(i):
        return 4 * c + i // 4, i % 4, source

    def is_me(tz, tx, tc):
        return jnp.logical_and(tz * 4 + tx == a, tc == c)

    def wave_copy(i):
        tz, tx, tc = wave_out(i)
        return remote(
            wsrc.at[i // 4, i % 4], wave.at[a % 16], w_send.at[i], w_recv.at[a % 16], d, tz, tx, tc
        )

    slot = x * 4 + z % 4

    def y_copies(step):
        to = (d + step) % 8
        return (
            remote(fac, fac_all.at[d, slot], y_send.at[0, step], y_recv.at[0, step], to, z, x, c),
            remote(ints, ints_all.at[d, slot], y_send.at[1, step], y_recv.at[1, step], to, z, x, c),
        )

    def z_copies(step):
        to = (z + step) % 8
        return to, [
            remote(whole.at[:, slot], whole.at[:, slot], z_send.at[kind, step], z_recv.at[kind, z % 4], d, to, x, c)
            for kind, whole in ((0, fac_all), (1, ints_all))
        ]

    def x_copies(step):
        to = (x + step) % 4
        column = pl.ds(4 * x, 4)
        return [
            remote(whole.at[:, column], whole.at[:, column], x_send.at[kind, step], x_recv.at[kind, step], d, z, to, c)
            for kind, whole in ((0, fac_all), (1, ints_all))
        ]

    def ring_copy(way, step):
        if way == 0:
            level, to = (d - step + 8) % 8, (d + 1) % 8
        else:
            level, to = (d + step) % 8, (d + 7) % 8
        at = pool_all.at[level, half]
        return remote(at, at, p_send.at[way, step], p_recv.at[way, step], to, z, x, c)

    def share(way, step):
        level = (d - 1 - step + 8) % 8 if way == 0 else (d + 1 + step) % 8
        at = pool_all.at[level, half]
        return remote(at, at, q_send.at[way, step], q_recv.at[way, step], d, z, x, other)

    mine = pool.at[0, z % 3]
    here = pltpu.make_async_copy(mine, pool_all.at[d], l_sem.at[0])
    over = remote(mine, pool_all.at[d], q_send.at[1, 3], q_recv.at[1, 3], d, z, x, other)

    def edges(way, parity):
        own, theirs = ((64, 1088), (1024, 0))[way]
        return remote(
            field.at[parity, pl.ds(own, 64)], field.at[parity, pl.ds(theirs, 64)],
            h_send.at[parity, way], h_recv.at[parity, way], d, z, x, other,
        )

    barrier = pltpu.get_barrier_semaphore()

    def greet(d, z, x, c):
        pl.semaphore_signal(barrier, inc=1, device_id=(d, z * 4 + x, c), device_id_type=MESH)

    greet(d, z, x, other)
    for i in range(1, 8):
        greet((d + i) % 8, z, x, c)
        greet(d, (z + i) % 8, x, c)
    for i in range(1, 4):
        greet(d, z, (x + i) % 4, c)

    @pl.loop(0, 12)
    def _(i):
        @pl.when(jnp.logical_not(is_me(*wave_out(i))))
        def _():
            greet(d, *wave_out(i))

    @pl.when(active)
    def _():
        @pl.loop(0, 16)
        def _(i):
            @pl.when(jnp.logical_not(is_me(*wave_in(i))))
            def _():
                greet(d, *wave_in(i))

    loops = jnp.logical_and(gives, near).astype(jnp.int32)
    pl.semaphore_wait(barrier, 18 + 12 - loops + jnp.where(active, 16 - loops, 0))

    @pl.when(gives)
    def _():
        over.start()
        here.start()

    @pl.when(near)
    def _():
        fac_all[d, slot] = fac[...]
        ints_all[d, slot] = ints[...]
        for step in range(1, 8):
            for copy in y_copies(step):
                copy.start()

    @pl.loop(0, 12)
    def _(i):
        same = is_me(*wave_out(i))

        @pl.when(same)
        def _():
            pltpu.make_async_copy(wsrc.at[i // 4, i % 4], wave.at[a % 16], l_sem.at[1]).start()

        @pl.when(jnp.logical_not(same))
        def _():
            wave_copy(i).start()

    @pl.when(gives)
    def _():
        here.wait()

    @pl.when(takes)
    def _():
        over.wait_recv()

    @pl.when(active)
    def _():
        ring_copy(0, 0).start()
        ring_copy(1, 0).start()

    @pl.when(near)
    def _():
        for step in range(1, 8):
            for copy in y_copies(step):
                copy.wait_recv()
        for step in range(1, 8):
            to, copies = z_copies(step)

            @pl.when(to < 6)
            def _():
                for copy in copies:
                    copy.start()

    def ring_step(step):
        for way in range(2):
            if step < 4 - way:
                ring_copy(way, step).wait_recv()
                if step < 3 - way:
                    ring_copy(way, step + 1).start()
                share(way, step).start()

    @pl.when(active)
    def _():
        ring_step(0)

        @pl.loop(0, 16)
        def _(i):
            same = is_me(*wave_in(i))

            @pl.when(same)
            def _():
                arrival(wave.at[i], l_sem.at[1]).wait()

            @pl.when(jnp.logical_not(same))
            def _():
                arrival(wave.at[i], w_recv.at[i]).wait()

            at = pl.ds(pl.multiple_of(64 + 64 * i, 64), 64)
            rows = wave[i]
            field[0, at, :128] = rows
            field[0, at, 128:] = turned(rows.astype(F32)).astype(BF)

        edges(0, 0).start()
        edges(1, 0).start()
        prod[DEAD] = jnp.zeros((8, 128), F32)

        for k in range(4):
            @pl.when(4 * c + k != z)
            def _():
                for kind, whole in ((0, fac_all), (1, ints_all)):
                    arrival(whole.at[:, 4 * x + k], z_recv.at[kind, k]).wait()
        for step in range(1, 4):
            for copy in x_copies(step):
                copy.start()

        ring_step(1)
        for step in range(1, 4):
            for copy in x_copies(step):
                copy.wait_recv()
        to_scalars = pltpu.make_async_copy(ints_all, lists, l_sem.at[2])
        to_scalars.start()
        ring_step(2)
        ring_step(3)
        to_scalars.wait()
        for way in range(2):
            for step in range(4 - way):
                share(way, step).wait_recv()

        def image_copy(level, step):
            to = (x + step) % 4
            return remote(
                img.at[level, pl.ds(4 * to, 4)], in_x.at[step, level],
                i_send.at[level, step], i_recv.at[level, step], d, z, to, c,
            )

        def owner_copy(level, k):
            return remote(
                x_sum.at[level, k], in_yz.at[d, z], o_send.at[level, k], o_recv.at[d, z],
                level, 4 * c + k, x, c,
            )

        def is_owner(level, k):
            return jnp.logical_and(level == d, 4 * c + k == z)

        def hand_in(level):
            for step in range(1, 4):
                image_copy(level, step).wait_recv()
            x_sum[level] = (img[level, pl.ds(4 * x, 4)] + in_x[1, level]) + (
                in_x[2, level] + in_x[3, level]
            )
            for k in range(4):
                @pl.when(is_owner(level, k))
                def _():
                    in_yz[d, z] = x_sum[level, k]

                @pl.when(jnp.logical_not(is_owner(level, k)))
                def _():
                    owner_copy(level, k).start()

        def group(level, now, g):
            later = 1 - now
            for m in range(8):
                new = []
                for r in (2 * m, 2 * m + 1):
                    block = 2 * g + r // 8
                    at = (block % 4) * 4 + block // 4
                    parts = [prod[lists[level, at, 0, k * 8 + r % 8]] for k in range(10)]
                    while len(parts) > 1:
                        parts = [sum(parts[i + 1 : i + 2], parts[i]) for i in range(0, len(parts), 2)]
                    row = parts[0] * fac_all[level, at, r % 8 : r % 8 + 1, :]
                    img[level, at, r % 8 : r % 8 + 1, :] = jnp.sum(row * row, axis=0, keepdims=True)
                    new.append(row)
                pair = jnp.concatenate(new, 0)
                at = pl.ds(pl.multiple_of(64 + 128 * g + 16 * m, 16), 16)
                field[later, at, :128] = pair.astype(BF)
                field[later, at, 128:] = turned(pair).astype(BF)

        @pl.loop(0, 8)
        def _(level):
            now = level % 2
            for way in range(2):
                edges(way, now).wait()
            for p in range(4):
                b0, b1 = pool_all[level, 2 * p], pool_all[level, 2 * p + 1]
                weights = jnp.concatenate(
                    [
                        jnp.concatenate([b0[:, :128], b1[:, :128]], 1),
                        jnp.concatenate([b0[:, 128:], b1[:, 128:]], 1),
                    ],
                    0,
                )
                product = jnp.dot(field[now], weights, preferred_element_type=F32)
                for k in range(2):
                    prod[pl.ds((2 * p + k) * WIDE, WIDE)] = product[
                        :, 128 * k : 128 * k + 128
                    ].reshape(WIDE, 8, 128)

            @pl.loop(0, 2)
            def _(i):
                group(level, now, 7 * i)

            @pl.when(level < 7)
            def _():
                for way in range(2):
                    edges(way, 1 - now).start()

            @pl.loop(1, 7)
            def _(g):
                group(level, now, g)

            for step in range(1, 4):
                image_copy(level, step).start()

            @pl.when(level > 0)
            def _():
                hand_in(level - 1)

        hand_in(7)

        @pl.loop(0, 8)
        def _(level):
            for step in range(1, 4):
                image_copy(level, step).wait_send()
            for k in range(4):
                @pl.when(jnp.logical_not(is_owner(level, k)))
                def _():
                    owner_copy(level, k).wait_send()

    echo = remote(done, got, e_sem.at[0], e_sem.at[1], d, z, x, other)

    @pl.when(near)
    def _():
        def add(i, total):
            fd, fz = i // 6, i % 6

            @pl.when(jnp.logical_or(fd != d, fz != z))
            def _():
                arrival(in_yz.at[fd, fz], o_recv.at[fd, fz]).wait()

            return total + in_yz[fd, fz]

        done[...] = lax.fori_loop(0, 48, add, jnp.zeros((8, 128), F32)) / 768.0
        echo.start()
        out[...] = done[...]
        echo.wait_send()

    @pl.when(jnp.logical_not(near))
    def _():
        echo.wait_recv()
        out[...] = got[...]

    @pl.when(near)
    def _():
        for step in range(1, 8):
            for copy in y_copies(step):
                copy.wait_send()
            to, copies = z_copies(step)

            @pl.when(to < 6)
            def _():
                for copy in copies:
                    copy.wait_send()

    @pl.loop(0, 12)
    def _(i):
        @pl.when(jnp.logical_not(is_me(*wave_out(i))))
        def _():
            wave_copy(i).wait_send()

    @pl.when(gives)
    def _():
        over.wait_send()

    @pl.when(active)
    def _():
        for step in range(1, 4):
            for copy in x_copies(step):
                copy.wait_send()
        for way in range(2):
            for step in range(4 - way):
                ring_copy(way, step).wait_send()
                share(way, step).wait_send()


def run(wsrc, fac, ints, pool):
    dma = pltpu.SemaphoreType.DMA
    vmem = pltpu.VMEM
    return pl.pallas_call(
        kernel,
        out_shape=jax.ShapeDtypeStruct((8, 128), F32),
        in_specs=[VMEM, VMEM, VMEM, ANY],
        out_specs=VMEM,
        scratch_shapes=[
            vmem((16, 64, 128), BF),
            vmem((2, 8 * WIDE, 256), BF),
            vmem((8, 8, 128, 256), BF),
            vmem((8, 16, 8, 128), F32),
            vmem((8, 16, 1, 128), jnp.int32),
            pltpu.SMEM((8, 16, 1, 128), jnp.int32),
            vmem((DEAD + 1, 8, 128), F32),
            vmem((8, 16, 8, 128), F32),
            vmem((4, 8, 4, 8, 128), F32),
            vmem((8, 4, 8, 128), F32),
            vmem((8, 8, 8, 128), F32),
            vmem((8, 128), F32),
            vmem((8, 128), F32),
            dma((3,)), dma((12,)), dma((16,)),
            dma((2, 8)), dma((2, 8)), dma((2, 8)), dma((2, 4)), dma((2, 4)), dma((2, 4)),
            dma((2, 4)), dma((2, 4)), dma((2, 4)), dma((2, 4)),
            dma((2, 2)), dma((2, 2)), dma((8, 4)), dma((8, 4)), dma((8, 4)), dma((8, 8)), dma((2,)),
        ],
        compiler_params=pltpu.CompilerParams(
            has_side_effects=True, collective_id=1, vmem_limit_bytes=48 * 2**20
        ),
        name="levels",
    )(wsrc, fac, ints, pool)


def per_device(surface, refl, pool, tile_ids, block_ids, counts):
    d = lax.axis_index("depth")
    first = 128 * (lax.axis_index("lat") // 16)
    own = lax.dynamic_slice_in_dim(surface, d * 16, 16, 2)
    own = own.reshape(3, 2, 4, 4, 8, 128)
    wsrc = jnp.transpose(own, (0, 2, 4, 3, 1, 5)).reshape(3, 4, 64, 128)
    scale = 1.0 / jnp.sqrt(counts[0].astype(F32))
    fac = (1.0 - refl.reshape(8, 128)) * scale[:, None]
    live = jnp.arange(10)[None, :] < counts[0][:, None]
    slots = jnp.where(live, block_ids[0] * WIDE + (tile_ids[0] - first + 8) % 256, DEAD)
    ints = jnp.concatenate([slots.T.reshape(1, 80), jnp.zeros((1, 48), jnp.int32)], 1)
    return run(wsrc, fac, ints.astype(jnp.int32), pool).reshape(1, 1024)


def solution(mesh):
    placed = (
        P("freq", None, None, "lat"),
        P("depth", "lat"),
        P("depth", "freq", None, None, None),
        P("depth", "lat", None),
        P("depth", "lat", None),
        P("depth", "lat"),
    )
    return jax.shard_map(
        per_device, mesh=mesh, in_specs=placed, out_specs=P("depth", "lat"), check_vma=False
    )
```

```python
import jax
import jax.numpy as jnp
from jax import lax
from jax.experimental import pallas as pl
from jax.experimental.pallas import tpu as pltpu
from jax.sharding import PartitionSpec as P

MESH = pl.DeviceIdType.MESH
ANY = pl.BlockSpec(memory_space=pl.ANY)
VMEM = pl.BlockSpec(memory_space=pltpu.VMEM)
BF = jnp.bfloat16
F32 = jnp.float32
WIDE = 144
DEAD = 8 * WIDE


def remote(src, dst, send, recv, d, z, x, c):
    return pltpu.make_async_remote_copy(
        src_ref=src,
        dst_ref=dst,
        send_sem=send,
        recv_sem=recv,
        device_id=(d, z * 4 + x, c),
        device_id_type=MESH,
    )


def arrival(ref, sem):
    return pltpu.make_async_copy(ref, ref, sem)


def turned(rows):
    count = rows.shape[0]
    even = lax.broadcasted_iota(jnp.int32, rows.shape, 0) % 2 == 0
    return jnp.where(even, -pltpu.roll(rows, count - 1, 0), pltpu.roll(rows, 1, 0))


def kernel(
    wsrc, refl, scale, ints, pool, out,
    fac_y, ints_y, wave, field, pool_all, fac_all, ints_all, lists, prod, img, in_x, x_sum, in_yz, done, got,
    l_sem, w_send, w_recv, y_send, y_recv, m_send, m_recv,
    p_send, p_recv, q_send, q_recv, h_send, h_recv, i_send, i_recv, o_send, o_recv, e_sem,
):
    d = lax.axis_index("depth")
    a = lax.axis_index("lat")
    c = lax.axis_index("freq")
    z, x = a // 4, a % 4
    other = 1 - c
    active = z < 6
    side = z // 4
    near = side == c
    source = z // 3
    gives = jnp.logical_and(active, c == source)
    takes = jnp.logical_and(active, c != source)

    def wave_out(i):
        return 3 * c + i // 4, i % 4, side

    def wave_in(i):
        return 4 * c + i // 4, i % 4, source

    def is_me(tz, tx, tc):
        return jnp.logical_and(tz * 4 + tx == a, tc == c)

    def wave_copy(i):
        tz, tx, tc = wave_out(i)
        return remote(
            wsrc.at[i // 4, i % 4], wave.at[a % 16], w_send.at[i], w_recv.at[a % 16], d, tz, tx, tc
        )

    slot = x * 4 + z % 4

    def y_copies(step):
        to = (d + step) % 8
        return (
            remote(fac_y.at[d], fac_y.at[d], y_send.at[0, step], y_recv.at[0, step], to, z, x, c),
            remote(ints_y.at[d], ints_y.at[d], y_send.at[1, step], y_recv.at[1, step], to, z, x, c),
        )

    def list_copies(i):
        tz, tx, tc = wave_out(i)
        return [
            remote(column, whole.at[:, slot], m_send.at[kind, i], m_recv.at[kind, slot], d, tz, tx, tc)
            for kind, column, whole in ((0, fac_y, fac_all), (1, ints_y, ints_all))
        ]

    def ring_copy(way, step, part):
        if way == 0:
            level, to = (d - step + 8) % 8, (d + 1) % 8
        else:
            level, to = (d + step) % 8, (d + 7) % 8
        at = pool_all.at[level, pl.ds(4 * c + 2 * part, 2)]
        i = 2 * step + part
        return remote(at, at, p_send.at[way, i], p_recv.at[way, i], to, z, x, c)

    def share(way, step, part):
        level = (d - 1 - step + 8) % 8 if way == 0 else (d + 1 + step) % 8
        at = pool_all.at[level, pl.ds(4 * c + 2 * part, 2)]
        i = 2 * step + part
        return remote(at, at, q_send.at[way, i], q_recv.at[way, i], d, z, x, other)

    ring = [(way, step, part) for step in range(3) for part in range(2) for way in range(2)]
    ring += [(0, 3, 0), (1, 3, 1)]

    mine = pool.at[0, z % 3]
    here = pltpu.make_async_copy(mine, pool_all.at[d], l_sem.at[0])

    def over(k):
        blocks = pl.ds(4 * other if k == 0 else 4 * c, 4)
        return remote(
            mine.at[blocks], pool_all.at[d, blocks], l_sem.at[3 + k], l_sem.at[5 + k], d, z, x, other
        )

    def came_over(k):
        blocks = pl.ds(4 * c if k == 0 else 4 * other, 4)
        return arrival(pool_all.at[d, blocks], l_sem.at[5 + k])

    def edges(way, parity):
        own, theirs = ((64, 1088), (1024, 0))[way]
        return remote(
            field.at[parity, pl.ds(own, 64)], field.at[parity, pl.ds(theirs, 64)],
            h_send.at[parity, way], h_recv.at[parity, way], d, z, x, other,
        )

    barrier = pltpu.get_barrier_semaphore()

    def greet(d, z, x, c):
        pl.semaphore_signal(barrier, inc=1, device_id=(d, z * 4 + x, c), device_id_type=MESH)

    greet(d, z, x, other)
    for i in range(1, 8):
        greet((d + i) % 8, z, x, c)
    for i in range(1, 4):
        greet(d, z, (x + i) % 4, c)

    @pl.loop(0, 12)
    def _(i):
        @pl.when(jnp.logical_not(is_me(*wave_out(i))))
        def _():
            greet(d, *wave_out(i))

    @pl.when(active)
    def _():
        @pl.loop(0, 16)
        def _(i):
            @pl.when(jnp.logical_not(is_me(*wave_in(i))))
            def _():
                greet(d, *wave_in(i))

    loops = jnp.logical_and(gives, near).astype(jnp.int32)
    fac_y[d] = (1.0 - refl[...]) * scale[...]
    ints_y[d] = ints[...]

    @pl.when(gives)
    def _():
        here.start()

    pl.semaphore_wait(barrier, 11 + 12 - loops + jnp.where(active, 16 - loops, 0))

    @pl.when(gives)
    def _():
        over(0).start()
        over(1).start()

    for step in range(1, 8):
        for copy in y_copies(step):
            copy.start()

    @pl.when(gives)
    def _():
        here.wait()

    @pl.when(takes)
    def _():
        came_over(0).wait()

    @pl.when(active)
    def _():
        for part in range(2):
            ring_copy(0, 0, part).start()
            ring_copy(1, 0, part).start()

    @pl.loop(0, 12)
    def _(i):
        same = is_me(*wave_out(i))

        @pl.when(same)
        def _():
            pltpu.make_async_copy(wsrc.at[i // 4, i % 4], wave.at[a % 16], l_sem.at[1]).start()

        @pl.when(jnp.logical_not(same))
        def _():
            wave_copy(i).start()

    for step in range(1, 8):
        for copy in y_copies(step):
            copy.wait_recv()

    @pl.loop(0, 12)
    def _(i):
        @pl.when(jnp.logical_not(is_me(*wave_out(i))))
        def _():
            for copy in list_copies(i):
                copy.start()

    @pl.when(jnp.logical_and(gives, near))
    def _():
        fac_all[:, slot] = fac_y[...]
        ints_all[:, slot] = ints_y[...]

    def ring_steps(these):
        for way, step, part in these:
            ring_copy(way, step, part).wait_recv()
            if (way, step + 1, part) in ring:
                ring_copy(way, step + 1, part).start()
            share(way, step, part).start()

    @pl.when(active)
    def _():
        ring_steps(ring[:4])

        @pl.loop(0, 16)
        def _(i):
            same = is_me(*wave_in(i))

            @pl.when(same)
            def _():
                arrival(wave.at[i], l_sem.at[1]).wait()

            @pl.when(jnp.logical_not(same))
            def _():
                arrival(wave.at[i], w_recv.at[i]).wait()

            at = pl.ds(pl.multiple_of(64 + 64 * i, 64), 64)
            rows = wave[i]
            field[0, at, :128] = rows
            field[0, at, 128:] = turned(rows.astype(F32)).astype(BF)

        edges(0, 0).start()
        edges(1, 0).start()
        prod[pl.ds(8 * DEAD, 8), :] = jnp.zeros((8, 128), F32)
        ring_steps(ring[4:8])

        @pl.loop(0, 16)
        def _(i):
            @pl.when(jnp.logical_not(is_me(*wave_in(i))))
            def _():
                at = (i % 4) * 4 + i // 4
                arrival(fac_all.at[:, at], m_recv.at[0, at]).wait()
                arrival(ints_all.at[:, at], m_recv.at[1, at]).wait()

        to_scalars = pltpu.make_async_copy(ints_all, lists, l_sem.at[2])
        to_scalars.start()
        ring_steps(ring[8:])
        to_scalars.wait()

        @pl.when(takes)
        def _():
            came_over(1).wait()

        for copy in ring:
            share(*copy).wait_recv()

        batches = ((0, 4), (4, 3), (7, 1))

        def image_copy(batch, step):
            first, count = batches[batch]
            to = (x + step) % 4
            return remote(
                img.at[pl.ds(first, count), pl.ds(4 * to, 4)], in_x.at[step, pl.ds(first, count)],
                i_send.at[batch, step], i_recv.at[batch, step], d, z, to, c,
            )

        def owner_copy(level, k):
            return remote(
                x_sum.at[level, k], in_yz.at[d, z], o_send.at[level, k], o_recv.at[d],
                level, 4 * c + k, x, c,
            )

        def is_owner(level, k):
            return jnp.logical_and(level == d, 4 * c + k == z)

        def send_images(batch):
            for step in range(1, 4):
                image_copy(batch, step).start()

        def hand_in(batch):
            for step in range(1, 4):
                image_copy(batch, step).wait_recv()

            @pl.loop(batches[batch][0], sum(batches[batch]))
            def _(level):
                x_sum[level] = (img[level, pl.ds(4 * x, 4)] + in_x[1, level]) + (
                    in_x[2, level] + in_x[3, level]
                )
                for k in range(4):
                    @pl.when(is_owner(level, k))
                    def _():
                        in_yz[d, z] = x_sum[level, k]

                    @pl.when(jnp.logical_not(is_owner(level, k)))
                    def _():
                        owner_copy(level, k).start()

        def group(level, now, g):
            later = 1 - now
            for m in range(16):
                new = []
                for r in (2 * m, 2 * m + 1):
                    block = 4 * g + r // 8
                    at = (block % 4) * 4 + block // 4
                    parts = []
                    for k in range(10):
                        parts.append(prod[pl.ds(lists[level, at, 0, k * 8 + r % 8], 8), :])
                    while len(parts) > 1:
                        parts = [sum(parts[i + 1 : i + 2], parts[i]) for i in range(0, len(parts), 2)]
                    row = parts[0] * fac_all[level, at, r % 8 : r % 8 + 1, :]
                    img[level, at, r % 8 : r % 8 + 1, :] = jnp.sum(row * row, axis=0, keepdims=True)
                    new.append(row)
                pair = jnp.concatenate(new, 0)
                at = pl.ds(pl.multiple_of(64 + 256 * g + 16 * m, 16), 16)
                field[later, at, :128] = pair.astype(BF)
                field[later, at, 128:] = turned(pair).astype(BF)

        @pl.loop(0, 8)
        def _(level):
            now = level % 2
            for way in range(2):
                edges(way, now).wait()
            for p in range(4):
                b0, b1 = pool_all[level, 2 * p], pool_all[level, 2 * p + 1]
                weights = jnp.concatenate(
                    [
                        jnp.concatenate([b0[:, :128], b1[:, :128]], 1),
                        jnp.concatenate([b0[:, 128:], b1[:, 128:]], 1),
                    ],
                    0,
                )
                product = jnp.dot(field[now], weights, preferred_element_type=F32)
                for k in range(2):
                    rows = pl.ds((2 * p + k) * 8 * WIDE, 8 * WIDE)
                    prod[rows, :] = product[:, 128 * k : 128 * k + 128]

            @pl.loop(0, 2)
            def _(i):
                group(level, now, 3 * i)

            @pl.when(level < 7)
            def _():
                for way in range(2):
                    edges(way, 1 - now).start()

            @pl.loop(1, 3)
            def _(g):
                group(level, now, g)

            for batch in range(2):
                @pl.when(level == sum(batches[batch]) - 1)
                def _():
                    send_images(batch)

            @pl.when(level == 5)
            def _():
                hand_in(0)

        send_images(2)
        hand_in(1)
        hand_in(2)

        for batch in range(3):
            for step in range(1, 4):
                image_copy(batch, step).wait_send()

        @pl.loop(0, 8)
        def _(level):
            for k in range(4):
                @pl.when(jnp.logical_not(is_owner(level, k)))
                def _():
                    owner_copy(level, k).wait_send()

    echo = remote(done, got, e_sem.at[0], e_sem.at[1], d, z, x, other)

    @pl.when(near)
    def _():
        total = jnp.zeros((8, 128), F32)
        for fd in range(8):
            @pl.when(jnp.logical_and(active, d == fd))
            def _():
                arrival(in_yz.at[fd, pl.ds(0, 5)], o_recv.at[fd]).wait()

            @pl.when(jnp.logical_not(jnp.logical_and(active, d == fd)))
            def _():
                arrival(in_yz.at[fd, pl.ds(0, 6)], o_recv.at[fd]).wait()

        for fd in range(8):
            for fz in range(6):
                total = total + in_yz[fd, fz]
        done[...] = total / 768.0
        echo.start()
        out[...] = done[...]
        echo.wait_send()

    @pl.when(jnp.logical_not(near))
    def _():
        echo.wait_recv()
        out[...] = got[...]

    for step in range(1, 8):
        for copy in y_copies(step):
            copy.wait_send()

    @pl.loop(0, 12)
    def _(i):
        @pl.when(jnp.logical_not(is_me(*wave_out(i))))
        def _():
            wave_copy(i).wait_send()
            for copy in list_copies(i):
                copy.wait_send()

    @pl.when(gives)
    def _():
        over(0).wait_send()
        over(1).wait_send()

    @pl.when(active)
    def _():
        for copy in ring:
            ring_copy(*copy).wait_send()
            share(*copy).wait_send()


def run(wsrc, refl, scale, ints, pool):
    dma = pltpu.SemaphoreType.DMA
    vmem = pltpu.VMEM
    return pl.pallas_call(
        kernel,
        out_shape=jax.ShapeDtypeStruct((8, 128), F32),
        in_specs=[VMEM, VMEM, VMEM, VMEM, ANY],
        out_specs=VMEM,
        scratch_shapes=[
            vmem((8, 8, 128), F32),
            vmem((8, 1, 128), jnp.int32),
            vmem((16, 64, 128), BF),
            vmem((2, 8 * WIDE, 256), BF),
            vmem((8, 8, 128, 256), BF),
            vmem((8, 16, 8, 128), F32),
            vmem((8, 16, 1, 128), jnp.int32),
            pltpu.SMEM((8, 16, 1, 128), jnp.int32),
            vmem((8 * DEAD + 8, 128), F32),
            vmem((8, 16, 8, 128), F32),
            vmem((4, 8, 4, 8, 128), F32),
            vmem((8, 4, 8, 128), F32),
            vmem((8, 8, 8, 128), F32),
            vmem((8, 128), F32),
            vmem((8, 128), F32),
            dma((7,)), dma((12,)), dma((16,)), dma((2, 8)), dma((2, 8)), dma((2, 12)), dma((2, 16)),
            dma((2, 8)), dma((2, 8)), dma((2, 8)), dma((2, 8)),
            dma((2, 2)), dma((2, 2)), dma((3, 4)), dma((3, 4)), dma((8, 4)), dma((8,)), dma((2,)),
        ],
        compiler_params=pltpu.CompilerParams(
            has_side_effects=True, collective_id=1, vmem_limit_bytes=60 * 2**20
        ),
        name="levels",
    )(wsrc, refl, scale, ints, pool)


def per_device(surface, refl, pool, tile_ids, block_ids, counts):
    d = lax.axis_index("depth")
    first = 128 * (lax.axis_index("lat") // 16)
    own = lax.dynamic_slice_in_dim(surface, d * 16, 16, 2)
    own = own.reshape(3, 2, 4, 4, 8, 128)
    wsrc = jnp.transpose(own, (0, 2, 4, 3, 1, 5)).reshape(3, 4, 64, 128)
    scale = jnp.broadcast_to((1.0 / jnp.sqrt(counts[0].astype(F32)))[:, None], (8, 128))
    live = jnp.arange(10)[None, :] < counts[0][:, None]
    slots = 8 * jnp.where(live, block_ids[0] * WIDE + (tile_ids[0] - first + 8) % 256, DEAD)
    ints = jnp.concatenate([slots.T.reshape(1, 80), jnp.zeros((1, 48), jnp.int32)], 1)
    return run(wsrc, refl.reshape(8, 128), scale, ints.astype(jnp.int32), pool).reshape(1, 1024)


def solution(mesh):
    placed = (
        P("freq", None, None, "lat"),
        P("depth", "lat"),
        P("depth", "freq", None, None, None),
        P("depth", "lat", None),
        P("depth", "lat", None),
        P("depth", "lat"),
    )
    return jax.shard_map(
        per_device, mesh=mesh, in_specs=placed, out_specs=P("depth", "lat"), check_vma=False
    )
```

```python
import jax
import jax.numpy as jnp
from jax import lax
from jax.experimental import pallas as pl
from jax.experimental.pallas import tpu as pltpu
from jax.sharding import PartitionSpec as P

MESH = pl.DeviceIdType.MESH
ANY = pl.BlockSpec(memory_space=pl.ANY)
VMEM = pl.BlockSpec(memory_space=pltpu.VMEM)
BF = jnp.bfloat16
F32 = jnp.float32
WIDE = 144
DEAD = 8 * WIDE


def remote(src, dst, send, recv, d, z, x, c):
    return pltpu.make_async_remote_copy(
        src_ref=src,
        dst_ref=dst,
        send_sem=send,
        recv_sem=recv,
        device_id=(d, z * 4 + x, c),
        device_id_type=MESH,
    )


def arrival(ref, sem):
    return pltpu.make_async_copy(ref, ref, sem)


def turned(rows):
    count = rows.shape[0]
    even = lax.broadcasted_iota(jnp.int32, rows.shape, 0) % 2 == 0
    return jnp.where(even, -pltpu.roll(rows, count - 1, 0), pltpu.roll(rows, 1, 0))


def kernel(
    wsrc, refl, tiles, blocks, counts, pool, out,
    draft, fac_y, ints_y, wave, field, pool_all, fac_all, ints_all, lists, prod, img, in_x, x_sum, in_yz,
    l_sem, w_send, w_recv, y_send, y_recv, m_send, m_recv,
    f_send, p_send, p_recv, q_send, q_recv, h_send, h_recv, i_send, i_recv, o_send, o_recv,
):
    d = lax.axis_index("depth")
    a = lax.axis_index("lat")
    c = lax.axis_index("freq")
    z, x = a // 4, a % 4
    other = 1 - c
    active = z < 6
    side = z // 4
    near = side == c
    source = z // 3
    gives = jnp.logical_and(active, c == source)
    takes = jnp.logical_and(active, c != source)

    def wave_out(i):
        return 3 * c + i // 4, i % 4, side

    def wave_in(i):
        return 4 * c + i // 4, i % 4, source

    def is_me(tz, tx, tc):
        return jnp.logical_and(tz * 4 + tx == a, tc == c)

    def wave_copy(i):
        tz, tx, tc = wave_out(i)
        return remote(
            wsrc.at[i // 4, i % 4], wave.at[a % 16], w_send.at[i], w_recv.at[a % 16], d, tz, tx, tc
        )

    slot = x * 4 + z % 4

    def y_copies(step):
        to = (d + step) % 8
        return (
            remote(fac_y.at[d], fac_y.at[d], y_send.at[0, step], y_recv.at[0, step], to, z, x, c),
            remote(ints_y.at[d], ints_y.at[d], y_send.at[1, step], y_recv.at[1, step], to, z, x, c),
        )

    def list_copies(i):
        tz, tx, tc = wave_out(i)
        return [
            remote(column, whole.at[:, slot], m_send.at[kind, i], m_recv.at[kind, slot], d, tz, tx, tc)
            for kind, column, whole in ((0, fac_y, fac_all), (1, ints_y, ints_all))
        ]

    mine = pool.at[0, z % 3]

    def ring_copy(way, step, part):
        if way == 0:
            level, to = (d - step + 8) % 8, (d + 1) % 8
        else:
            level, to = (d + step) % 8, (d + 7) % 8
        at = pool_all.at[level, pl.ds(4 * c + 2 * part, 2)]
        i = 2 * step + part
        return remote(at, at, p_send.at[way, i], p_recv.at[way, i], to, z, x, c)

    def share(way, step, part):
        level = (d - 1 - step + 8) % 8 if way == 0 else (d + 1 + step) % 8
        at = pool_all.at[level, pl.ds(4 * c + 2 * part, 2)]
        i = 2 * step + part
        return remote(at, at, q_send.at[way, i], q_recv.at[way, i], d, z, x, other)

    def first_copy(way, part, tc):
        blocks_here = pl.ds(4 * tc + 2 * part, 2)
        to = (d + 1) % 8 if way == 0 else (d + 7) % 8
        return remote(
            mine.at[blocks_here], pool_all.at[d, blocks_here],
            f_send.at[way, 2 * part + (tc == c).astype(jnp.int32)], p_recv.at[way, part], to, z, x, tc,
        )

    ring = [(way, step, part) for step in range(3) for part in range(2) for way in range(2)]
    ring += [(0, 3, 0), (1, 3, 1)]

    here = pltpu.make_async_copy(mine, pool_all.at[d], l_sem.at[0])

    over = remote(mine, pool_all.at[d], l_sem.at[3], l_sem.at[4], d, z, x, other)

    def edges(way, parity):
        own, theirs = ((64, 1088), (1024, 0))[way]
        return remote(
            field.at[parity, pl.ds(own, 64)], field.at[parity, pl.ds(theirs, 64)],
            h_send.at[parity, way], h_recv.at[parity, way], d, z, x, other,
        )

    barrier = pltpu.get_barrier_semaphore()

    def greet(d, z, x, c):
        pl.semaphore_signal(barrier, inc=1, device_id=(d, z * 4 + x, c), device_id_type=MESH)

    greet(d, z, x, other)
    greet((d + 1) % 8, z, x, other)
    greet((d + 7) % 8, z, x, other)
    for i in range(1, 8):
        greet((d + i) % 8, z, x, c)
    for i in range(1, 4):
        greet(d, z, (x + i) % 4, c)

    @pl.loop(0, 12)
    def _(i):
        @pl.when(jnp.logical_not(is_me(*wave_out(i))))
        def _():
            greet(d, *wave_out(i))

    @pl.when(active)
    def _():
        @pl.loop(0, 16)
        def _(i):
            @pl.when(jnp.logical_not(is_me(*wave_in(i))))
            def _():
                greet(d, *wave_in(i))

    loops = jnp.logical_and(gives, near).astype(jnp.int32)
    lane = lax.broadcasted_iota(jnp.int32, (1, 128), 1)
    draft[...] = jnp.zeros((8, 128), jnp.int32)
    draft[:, :10] = 8 * (blocks[...] * WIDE + (tiles[...] - 128 * side + 8) % 256)
    line = jnp.zeros((1, 128), jnp.int32)
    for r in range(8):
        live = counts[0, r]
        fac_y[d, r : r + 1, :] = (1.0 - refl[r : r + 1, :]) * (
            1.0 / jnp.sqrt(jnp.full((1, 128), live, jnp.int32).astype(F32))
        )
        slots = jnp.where(lane < live, draft[r : r + 1, :], 8 * DEAD)
        slots = jnp.where(lane < 10, slots, 0)
        line = line + (slots if r == 0 else pltpu.roll(slots, 10 * r, 1))
    ints_y[d] = line

    @pl.when(gives)
    def _():
        here.start()

    pl.semaphore_wait(barrier, 13 + 12 - loops + jnp.where(active, 16 - loops, 0))

    @pl.when(gives)
    def _():
        for part in range(2):
            for tc in (c, other):
                for way in range(2):
                    first_copy(way, part, tc).start()
        over.start()

    for step in range(1, 8):
        for copy in y_copies(step):
            copy.start()

    @pl.loop(0, 12)
    def _(i):
        same = is_me(*wave_out(i))

        @pl.when(same)
        def _():
            pltpu.make_async_copy(wsrc.at[i // 4, i % 4], wave.at[a % 16], l_sem.at[1]).start()

        @pl.when(jnp.logical_not(same))
        def _():
            wave_copy(i).start()

    for step in range(1, 8):
        for copy in y_copies(step):
            copy.wait_recv()

    @pl.loop(0, 12)
    def _(i):
        @pl.when(jnp.logical_not(is_me(*wave_out(i))))
        def _():
            for copy in list_copies(i):
                copy.start()

    @pl.when(jnp.logical_and(gives, near))
    def _():
        fac_all[:, slot] = fac_y[...]
        ints_all[:, slot] = ints_y[...]

    def ring_steps(these):
        for way, step, part in these:
            ring_copy(way, step, part).wait_recv()
            if (way, step + 1, part) in ring:
                ring_copy(way, step + 1, part).start()
            share(way, step, part).start()

    @pl.when(active)
    def _():
        ring_steps(ring[:4])

        @pl.loop(0, 16)
        def _(i):
            same = is_me(*wave_in(i))

            @pl.when(same)
            def _():
                arrival(wave.at[i], l_sem.at[1]).wait()

            @pl.when(jnp.logical_not(same))
            def _():
                arrival(wave.at[i], w_recv.at[i]).wait()

            at = pl.ds(pl.multiple_of(64 + 64 * i, 64), 64)
            rows = wave[i]
            field[0, at, :128] = rows
            field[0, at, 128:] = turned(rows.astype(F32)).astype(BF)

        edges(0, 0).start()
        edges(1, 0).start()
        prod[pl.ds(8 * DEAD, 8), :] = jnp.zeros((8, 128), F32)
        ring_steps(ring[4:8])

        @pl.loop(0, 16)
        def _(i):
            @pl.when(jnp.logical_not(is_me(*wave_in(i))))
            def _():
                at = (i % 4) * 4 + i // 4
                arrival(fac_all.at[:, at], m_recv.at[0, at]).wait()
                arrival(ints_all.at[:, at], m_recv.at[1, at]).wait()

        to_scalars = pltpu.make_async_copy(ints_all, lists, l_sem.at[2])
        to_scalars.start()
        ring_steps(ring[8:])
        to_scalars.wait()

        @pl.when(gives)
        def _():
            here.wait()

        @pl.when(takes)
        def _():
            over.wait_recv()

        for copy in ring:
            share(*copy).wait_recv()

        batches = ((0, 4), (4, 3), (7, 1))

        def image_copy(batch, step):
            first, count = batches[batch]
            to = (x + step) % 4
            return remote(
                img.at[pl.ds(first, count), pl.ds(4 * to, 4)], in_x.at[step, pl.ds(first, count)],
                i_send.at[batch, step], i_recv.at[batch, step], d, z, to, c,
            )

        def owner_copy(level, k, tc):
            return remote(
                x_sum.at[level, k], in_yz.at[d, z], o_send.at[level, 2 * k + (tc == c).astype(jnp.int32)],
                o_recv.at[d], level, 4 * c + k, x, tc,
            )

        def is_owner(level, k):
            return jnp.logical_and(level == d, 4 * c + k == z)

        def send_images(batch):
            for step in range(1, 4):
                image_copy(batch, step).start()

        def hand_in(batch):
            for step in range(1, 4):
                image_copy(batch, step).wait_recv()

            @pl.loop(batches[batch][0], sum(batches[batch]))
            def _(level):
                x_sum[level] = (img[level, pl.ds(4 * x, 4)] + in_x[1, level]) + (
                    in_x[2, level] + in_x[3, level]
                )
                for k in range(4):
                    @pl.when(is_owner(level, k))
                    def _():
                        in_yz[d, z] = x_sum[level, k]

                    @pl.when(jnp.logical_not(is_owner(level, k)))
                    def _():
                        owner_copy(level, k, c).start()

                    owner_copy(level, k, other).start()

        def group(level, now, g):
            later = 1 - now
            for m in range(16):
                new = []
                for r in (2 * m, 2 * m + 1):
                    block = 4 * g + r // 8
                    at = (block % 4) * 4 + block // 4
                    parts = []
                    for k in range(10):
                        parts.append(prod[pl.ds(lists[level, at, 0, r % 8 * 10 + k], 8), :])
                    while len(parts) > 1:
                        parts = [sum(parts[i + 1 : i + 2], parts[i]) for i in range(0, len(parts), 2)]
                    row = parts[0] * fac_all[level, at, r % 8 : r % 8 + 1, :]
                    img[level, at, r % 8 : r % 8 + 1, :] = jnp.sum(row * row, axis=0, keepdims=True)
                    new.append(row)
                pair = jnp.concatenate(new, 0)
                at = pl.ds(pl.multiple_of(64 + 256 * g + 16 * m, 16), 16)
                field[later, at, :128] = pair.astype(BF)
                field[later, at, 128:] = turned(pair).astype(BF)

        @pl.loop(0, 8)
        def _(level):
            now = level % 2
            for way in range(2):
                edges(way, now).wait()
            for p in range(4):
                b0, b1 = pool_all[level, 2 * p], pool_all[level, 2 * p + 1]
                weights = jnp.concatenate(
                    [
                        jnp.concatenate([b0[:, :128], b1[:, :128]], 1),
                        jnp.concatenate([b0[:, 128:], b1[:, 128:]], 1),
                    ],
                    0,
                )
                product = jnp.dot(field[now], weights, preferred_element_type=F32)
                for k in range(2):
                    rows = pl.ds((2 * p + k) * 8 * WIDE, 8 * WIDE)
                    prod[rows, :] = product[:, 128 * k : 128 * k + 128]

            @pl.loop(0, 2)
            def _(i):
                group(level, now, 3 * i)

            @pl.when(level < 7)
            def _():
                for way in range(2):
                    edges(way, 1 - now).start()

            @pl.loop(1, 3)
            def _(g):
                group(level, now, g)

            for batch in range(2):
                @pl.when(level == sum(batches[batch]) - 1)
                def _():
                    send_images(batch)

            @pl.when(level == 5)
            def _():
                hand_in(0)

        send_images(2)
        hand_in(1)
        hand_in(2)

        for batch in range(3):
            for step in range(1, 4):
                image_copy(batch, step).wait_send()

        @pl.loop(0, 8)
        def _(level):
            for k in range(4):
                @pl.when(jnp.logical_not(is_owner(level, k)))
                def _():
                    owner_copy(level, k, c).wait_send()

                owner_copy(level, k, other).wait_send()

    own = jnp.logical_and(active, near)
    total = jnp.zeros((8, 128), F32)
    for fd in range(8):
        local = jnp.logical_and(own, d == fd)

        @pl.when(local)
        def _():
            arrival(in_yz.at[fd, pl.ds(0, 5)], o_recv.at[fd]).wait()

        @pl.when(jnp.logical_not(local))
        def _():
            arrival(in_yz.at[fd, pl.ds(0, 6)], o_recv.at[fd]).wait()

    for fd in range(8):
        for fz in range(6):
            total = total + in_yz[fd, fz]
    total = total / 768.0
    for r in range(8):
        out[:, 128 * r : 128 * r + 128] = total[r : r + 1, :]

    for step in range(1, 8):
        for copy in y_copies(step):
            copy.wait_send()

    @pl.loop(0, 12)
    def _(i):
        @pl.when(jnp.logical_not(is_me(*wave_out(i))))
        def _():
            wave_copy(i).wait_send()
            for copy in list_copies(i):
                copy.wait_send()

    @pl.when(gives)
    def _():
        over.wait_send()
        for part in range(2):
            for tc in (c, other):
                for way in range(2):
                    first_copy(way, part, tc).wait_send()

    @pl.when(active)
    def _():
        for way, step, part in ring:
            if step:
                ring_copy(way, step, part).wait_send()
            share(way, step, part).wait_send()


def run(wsrc, refl, tiles, blocks, counts, pool):
    dma = pltpu.SemaphoreType.DMA
    vmem = pltpu.VMEM
    return pl.pallas_call(
        kernel,
        out_shape=jax.ShapeDtypeStruct((1, 1024), F32),
        in_specs=[VMEM, VMEM, VMEM, VMEM, pl.BlockSpec(memory_space=pltpu.SMEM), ANY],
        out_specs=VMEM,
        scratch_shapes=[
            vmem((8, 128), jnp.int32),
            vmem((8, 8, 128), F32),
            vmem((8, 1, 128), jnp.int32),
            vmem((16, 64, 128), BF),
            vmem((2, 8 * WIDE, 256), BF),
            vmem((8, 8, 128, 256), BF),
            vmem((8, 16, 8, 128), F32),
            vmem((8, 16, 1, 128), jnp.int32),
            pltpu.SMEM((8, 16, 1, 128), jnp.int32),
            vmem((8 * DEAD + 8, 128), F32),
            vmem((8, 16, 8, 128), F32),
            vmem((4, 8, 4, 8, 128), F32),
            vmem((8, 4, 8, 128), F32),
            vmem((8, 8, 8, 128), F32),
            dma((5,)), dma((12,)), dma((16,)), dma((2, 8)), dma((2, 8)), dma((2, 12)), dma((2, 16)),
            dma((2, 4)), dma((2, 8)), dma((2, 8)), dma((2, 8)), dma((2, 8)),
            dma((2, 2)), dma((2, 2)), dma((3, 4)), dma((3, 4)), dma((8, 8)), dma((8,)),
        ],
        compiler_params=pltpu.CompilerParams(
            has_side_effects=True, collective_id=1, vmem_limit_bytes=60 * 2**20
        ),
        name="levels",
    )(wsrc, refl, tiles, blocks, counts, pool)


def per_device(surface, refl, pool, tile_ids, block_ids, counts):
    d = lax.axis_index("depth")
    own = lax.dynamic_slice_in_dim(surface, d * 16, 16, 2)
    own = own.reshape(3, 2, 4, 4, 8, 128)
    wsrc = jnp.transpose(own, (0, 2, 4, 3, 1, 5)).reshape(3, 4, 64, 128)
    return run(wsrc, refl.reshape(8, 128), tile_ids[0], block_ids[0], counts, pool)


def solution(mesh):
    placed = (
        P("freq", None, None, "lat"),
        P("depth", "lat"),
        P("depth", "freq", None, None, None),
        P("depth", "lat", None),
        P("depth", "lat", None),
        P("depth", "lat"),
    )
    return jax.shard_map(
        per_device, mesh=mesh, in_specs=placed, out_specs=P("depth", "lat"), check_vma=False
    )
```

```python
import jax
import jax.numpy as jnp
from jax import lax
from jax.experimental import pallas as pl
from jax.experimental.pallas import tpu as pltpu
from jax.sharding import PartitionSpec as P

MESH = pl.DeviceIdType.MESH
ANY = pl.BlockSpec(memory_space=pl.ANY)
VMEM = pl.BlockSpec(memory_space=pltpu.VMEM)
BF = jnp.bfloat16
F32 = jnp.float32
WIDE = 144
DEAD = 8 * WIDE


def remote(src, dst, send, recv, d, z, x, c):
    return pltpu.make_async_remote_copy(
        src_ref=src,
        dst_ref=dst,
        send_sem=send,
        recv_sem=recv,
        device_id=(d, z * 4 + x, c),
        device_id_type=MESH,
    )


def arrival(ref, sem):
    return pltpu.make_async_copy(ref, ref, sem)


def turned(rows):
    count = rows.shape[0]
    even = lax.broadcasted_iota(jnp.int32, rows.shape, 0) % 2 == 0
    return jnp.where(even, -pltpu.roll(rows, count - 1, 0), pltpu.roll(rows, 1, 0))


def kernel(
    surface, refl, tiles, blocks, counts, pool, out,
    raw, mixed, wsrc, draft, fac_y, ints_y, wave, field, pool_all, fac_all, ints_all, lists, prod, img, in_x, x_sum, in_yz,
    l_sem, w_send, w_recv, y_send, y_recv, m_send, m_recv,
    f_send, p_send, p_recv, q_send, q_recv, h_send, h_recv, i_send, i_recv, o_send, o_recv,
):
    d = lax.axis_index("depth")
    a = lax.axis_index("lat")
    c = lax.axis_index("freq")
    z, x = a // 4, a % 4
    other = 1 - c
    active = z < 6
    side = z // 4
    near = side == c
    source = z // 3
    gives = jnp.logical_and(active, c == source)
    takes = jnp.logical_and(active, c != source)

    def wave_out(i):
        return 3 * c + i // 4, i % 4, side

    def wave_in(i):
        return 4 * c + i // 4, i % 4, source

    def is_me(tz, tx, tc):
        return jnp.logical_and(tz * 4 + tx == a, tc == c)

    def wave_copy(i):
        tz, tx, tc = wave_out(i)
        return remote(
            wsrc.at[i // 4, i % 4], wave.at[a % 16], w_send.at[i], w_recv.at[a % 16], d, tz, tx, tc
        )

    slot = x * 4 + z % 4

    def y_copies(step):
        to = (d + step) % 8
        return (
            remote(fac_y.at[d], fac_y.at[d], y_send.at[0, step], y_recv.at[0, step], to, z, x, c),
            remote(ints_y.at[d], ints_y.at[d], y_send.at[1, step], y_recv.at[1, step], to, z, x, c),
        )

    def list_copies(i):
        tz, tx, tc = wave_out(i)
        return [
            remote(column, whole.at[:, slot], m_send.at[kind, i], m_recv.at[kind, slot], d, tz, tx, tc)
            for kind, column, whole in ((0, fac_y, fac_all), (1, ints_y, ints_all))
        ]

    mine = pool.at[0, z % 3]

    def ring_copy(way, step, part):
        if way == 0:
            level, to = (d - step + 8) % 8, (d + 1) % 8
        else:
            level, to = (d + step) % 8, (d + 7) % 8
        at = pool_all.at[level, pl.ds(4 * c + 2 * part, 2)]
        i = 2 * step + part
        return remote(at, at, p_send.at[way, i], p_recv.at[way, i], to, z, x, c)

    def share(way, step, part):
        level = (d - 1 - step + 8) % 8 if way == 0 else (d + 1 + step) % 8
        at = pool_all.at[level, pl.ds(4 * c + 2 * part, 2)]
        i = 2 * step + part
        return remote(at, at, q_send.at[way, i], q_recv.at[way, i], d, z, x, other)

    def first_copy(way, part, tc):
        blocks_here = pl.ds(4 * tc + 2 * part, 2)
        to = (d + 1) % 8 if way == 0 else (d + 7) % 8
        return remote(
            mine.at[blocks_here], pool_all.at[d, blocks_here],
            f_send.at[way, 2 * part + (tc == c).astype(jnp.int32)], p_recv.at[way, part], to, z, x, tc,
        )

    ring = [(way, step, part) for step in range(3) for part in range(2) for way in range(2)]
    ring += [(0, 3, 0), (1, 3, 1)]

    here = pltpu.make_async_copy(mine, pool_all.at[d], l_sem.at[0])

    over = remote(mine, pool_all.at[d], l_sem.at[3], l_sem.at[4], d, z, x, other)

    def edges(way, parity):
        own, theirs = ((64, 1088), (1024, 0))[way]
        return remote(
            field.at[parity, pl.ds(own, 64)], field.at[parity, pl.ds(theirs, 64)],
            h_send.at[parity, way], h_recv.at[parity, way], d, z, x, other,
        )

    barrier = pltpu.get_barrier_semaphore()

    def greet(d, z, x, c):
        pl.semaphore_signal(barrier, inc=1, device_id=(d, z * 4 + x, c), device_id_type=MESH)

    greet(d, z, x, other)
    greet((d + 1) % 8, z, x, other)
    greet((d + 7) % 8, z, x, other)
    for i in range(1, 8):
        greet((d + i) % 8, z, x, c)
    for i in range(1, 4):
        greet(d, z, (x + i) % 4, c)

    @pl.loop(0, 12)
    def _(i):
        @pl.when(jnp.logical_not(is_me(*wave_out(i))))
        def _():
            greet(d, *wave_out(i))

    @pl.when(active)
    def _():
        @pl.loop(0, 16)
        def _(i):
            @pl.when(jnp.logical_not(is_me(*wave_in(i))))
            def _():
                greet(d, *wave_in(i))

    loops = jnp.logical_and(gives, near).astype(jnp.int32)
    fetch = pltpu.make_async_copy(surface.at[:, :, pl.ds(16 * d, 16), :], raw, l_sem.at[5])
    fetch.start()

    @pl.when(gives)
    def _():
        here.start()

    lane = lax.broadcasted_iota(jnp.int32, (1, 128), 1)
    draft[...] = jnp.zeros((8, 128), jnp.int32)
    draft[:, :10] = 8 * (blocks[...] * WIDE + (tiles[...] - 128 * side + 8) % 256)
    line = jnp.zeros((1, 128), jnp.int32)
    for r in range(8):
        live = counts[0, r]
        fac_y[d, r : r + 1, :] = (1.0 - refl[r : r + 1, :]) * (
            1.0 / jnp.sqrt(jnp.full((1, 128), live, jnp.int32).astype(F32))
        )
        slots = jnp.where(lane < live, draft[r : r + 1, :], 8 * DEAD)
        slots = jnp.where(lane < 10, slots, 0)
        line = line + (slots if r == 0 else pltpu.roll(slots, 10 * r, 1))
    ints_y[d] = line

    fetch.wait()

    @pl.loop(0, 3)
    def _(f):
        for part in range(2):
            rows = raw[f, part].astype(F32)
            for tx in range(4):
                for t in range(8):
                    at = pl.ds(256 * f + 64 * tx + 8 * t + part, 4, stride=2)
                    mixed[at, :] = rows[4 * tx : 4 * tx + 4, 128 * t : 128 * t + 128]
        for tx in range(4):
            at = pl.ds(pl.multiple_of(256 * f + 64 * tx, 64), 64)
            wsrc[f, tx] = mixed[at, :].astype(BF)

    pl.semaphore_wait(barrier, 13 + 12 - loops + jnp.where(active, 16 - loops, 0))

    @pl.when(gives)
    def _():
        for part in range(2):
            for tc in (c, other):
                for way in range(2):
                    first_copy(way, part, tc).start()
        over.start()

    for step in range(1, 8):
        for copy in y_copies(step):
            copy.start()

    @pl.loop(0, 12)
    def _(i):
        same = is_me(*wave_out(i))

        @pl.when(same)
        def _():
            pltpu.make_async_copy(wsrc.at[i // 4, i % 4], wave.at[a % 16], l_sem.at[1]).start()

        @pl.when(jnp.logical_not(same))
        def _():
            wave_copy(i).start()

    for step in range(1, 8):
        for copy in y_copies(step):
            copy.wait_recv()

    @pl.loop(0, 12)
    def _(i):
        @pl.when(jnp.logical_not(is_me(*wave_out(i))))
        def _():
            for copy in list_copies(i):
                copy.start()

    @pl.when(jnp.logical_and(gives, near))
    def _():
        fac_all[:, slot] = fac_y[...]
        ints_all[:, slot] = ints_y[...]

    def ring_steps(these):
        for way, step, part in these:
            ring_copy(way, step, part).wait_recv()
            if (way, step + 1, part) in ring:
                ring_copy(way, step + 1, part).start()
            share(way, step, part).start()

    @pl.when(active)
    def _():
        ring_steps(ring[:4])

        @pl.loop(0, 16)
        def _(i):
            same = is_me(*wave_in(i))

            @pl.when(same)
            def _():
                arrival(wave.at[i], l_sem.at[1]).wait()

            @pl.when(jnp.logical_not(same))
            def _():
                arrival(wave.at[i], w_recv.at[i]).wait()

            at = pl.ds(pl.multiple_of(64 + 64 * i, 64), 64)
            rows = wave[i]
            field[0, at, :128] = rows
            field[0, at, 128:] = turned(rows.astype(F32)).astype(BF)

        edges(0, 0).start()
        edges(1, 0).start()
        prod[pl.ds(8 * DEAD, 8), :] = jnp.zeros((8, 128), F32)
        ring_steps(ring[4:12])

        @pl.loop(0, 16)
        def _(i):
            @pl.when(jnp.logical_not(is_me(*wave_in(i))))
            def _():
                at = (i % 4) * 4 + i // 4
                arrival(fac_all.at[:, at], m_recv.at[0, at]).wait()
                arrival(ints_all.at[:, at], m_recv.at[1, at]).wait()

        to_scalars = pltpu.make_async_copy(ints_all, lists, l_sem.at[2])
        to_scalars.start()
        ring_steps(ring[12:])
        to_scalars.wait()

        @pl.when(gives)
        def _():
            here.wait()

        @pl.when(takes)
        def _():
            over.wait_recv()

        for copy in ring:
            share(*copy).wait_recv()

        batches = ((0, 3), (3, 3), (6, 1), (7, 1))

        def image_copy(batch, step):
            first, count = batches[batch]
            to = (x + step) % 4
            return remote(
                img.at[pl.ds(first, count), pl.ds(4 * to, 4)], in_x.at[step, pl.ds(first, count)],
                i_send.at[batch, step], i_recv.at[batch, step], d, z, to, c,
            )

        def owner_copy(level, k, tc):
            return remote(
                x_sum.at[level, k], in_yz.at[d, z], o_send.at[level, 2 * k + (tc == c).astype(jnp.int32)],
                o_recv.at[d], level, 4 * c + k, x, tc,
            )

        def is_owner(level, k):
            return jnp.logical_and(level == d, 4 * c + k == z)

        def send_images(batch):
            for step in range(1, 4):
                image_copy(batch, step).start()

        def hand_in(batch):
            for step in range(1, 4):
                image_copy(batch, step).wait_recv()

            @pl.loop(batches[batch][0], sum(batches[batch]))
            def _(level):
                x_sum[level] = (img[level, pl.ds(4 * x, 4)] + in_x[1, level]) + (
                    in_x[2, level] + in_x[3, level]
                )
                for k in range(4):
                    @pl.when(is_owner(level, k))
                    def _():
                        in_yz[d, z] = x_sum[level, k]

                    @pl.when(jnp.logical_not(is_owner(level, k)))
                    def _():
                        owner_copy(level, k, c).start()

                    owner_copy(level, k, other).start()

        def group(level, now, g):
            later = 1 - now
            for m in range(16):
                new = []
                for r in (2 * m, 2 * m + 1):
                    block = 4 * g + r // 8
                    at = (block % 4) * 4 + block // 4
                    parts = []
                    for k in range(10):
                        parts.append(prod[pl.ds(lists[level, at, 0, r % 8 * 10 + k], 8), :])
                    while len(parts) > 1:
                        parts = [sum(parts[i + 1 : i + 2], parts[i]) for i in range(0, len(parts), 2)]
                    row = parts[0] * fac_all[level, at, r % 8 : r % 8 + 1, :]
                    img[level, at, r % 8 : r % 8 + 1, :] = jnp.sum(row * row, axis=0, keepdims=True)
                    new.append(row)
                pair = jnp.concatenate(new, 0)
                at = pl.ds(pl.multiple_of(64 + 256 * g + 16 * m, 16), 16)
                field[later, at, :128] = pair.astype(BF)
                field[later, at, 128:] = turned(pair).astype(BF)

        @pl.loop(0, 8)
        def _(level):
            now = level % 2
            for way in range(2):
                edges(way, now).wait()
            for p in range(4):
                b0, b1 = pool_all[level, 2 * p], pool_all[level, 2 * p + 1]
                weights = jnp.concatenate(
                    [
                        jnp.concatenate([b0[:, :128], b1[:, :128]], 1),
                        jnp.concatenate([b0[:, 128:], b1[:, 128:]], 1),
                    ],
                    0,
                )
                product = jnp.dot(field[now], weights, preferred_element_type=F32)
                for k in range(2):
                    rows = pl.ds((2 * p + k) * 8 * WIDE, 8 * WIDE)
                    prod[rows, :] = product[:, 128 * k : 128 * k + 128]

            @pl.loop(0, 2)
            def _(i):
                group(level, now, 3 * i)

            @pl.when(level < 7)
            def _():
                for way in range(2):
                    edges(way, 1 - now).start()

            @pl.loop(1, 3)
            def _(g):
                group(level, now, g)

            for batch in range(4):
                @pl.when(level == sum(batches[batch]) - 1)
                def _():
                    send_images(batch)

            for batch in range(2):
                @pl.when(level == 4 + 2 * batch)
                def _():
                    hand_in(batch)

        hand_in(2)
        hand_in(3)

        for batch in range(4):
            for step in range(1, 4):
                image_copy(batch, step).wait_send()

        @pl.loop(0, 8)
        def _(level):
            for k in range(4):
                @pl.when(jnp.logical_not(is_owner(level, k)))
                def _():
                    owner_copy(level, k, c).wait_send()

                owner_copy(level, k, other).wait_send()

    own = jnp.logical_and(active, near)
    total = jnp.zeros((8, 128), F32)
    for fd in range(8):
        local = jnp.logical_and(own, d == fd)

        @pl.when(local)
        def _():
            arrival(in_yz.at[fd, pl.ds(0, 5)], o_recv.at[fd]).wait()

        @pl.when(jnp.logical_not(local))
        def _():
            arrival(in_yz.at[fd, pl.ds(0, 6)], o_recv.at[fd]).wait()

    for fd in range(8):
        for fz in range(6):
            total = total + in_yz[fd, fz]
    out[...] = total

    for step in range(1, 8):
        for copy in y_copies(step):
            copy.wait_send()

    @pl.loop(0, 12)
    def _(i):
        @pl.when(jnp.logical_not(is_me(*wave_out(i))))
        def _():
            wave_copy(i).wait_send()
            for copy in list_copies(i):
                copy.wait_send()

    @pl.when(gives)
    def _():
        over.wait_send()
        for part in range(2):
            for tc in (c, other):
                for way in range(2):
                    first_copy(way, part, tc).wait_send()

    @pl.when(active)
    def _():
        for way, step, part in ring:
            if step:
                ring_copy(way, step, part).wait_send()
            share(way, step, part).wait_send()


def run(surface, refl, tiles, blocks, counts, pool):
    dma = pltpu.SemaphoreType.DMA
    vmem = pltpu.VMEM
    return pl.pallas_call(
        kernel,
        out_shape=jax.ShapeDtypeStruct((8, 128), F32),
        in_specs=[ANY, VMEM, VMEM, VMEM, pl.BlockSpec(memory_space=pltpu.SMEM), ANY],
        out_specs=VMEM,
        scratch_shapes=[
            vmem((3, 2, 16, 1024), BF),
            vmem((768, 128), F32),
            vmem((3, 4, 64, 128), BF),
            vmem((8, 128), jnp.int32),
            vmem((8, 8, 128), F32),
            vmem((8, 1, 128), jnp.int32),
            vmem((16, 64, 128), BF),
            vmem((2, 8 * WIDE, 256), BF),
            vmem((8, 8, 128, 256), BF),
            vmem((8, 16, 8, 128), F32),
            vmem((8, 16, 1, 128), jnp.int32),
            pltpu.SMEM((8, 16, 1, 128), jnp.int32),
            vmem((8 * DEAD + 8, 128), F32),
            vmem((8, 16, 8, 128), F32),
            vmem((4, 8, 4, 8, 128), F32),
            vmem((8, 4, 8, 128), F32),
            vmem((8, 8, 8, 128), F32),
            dma((6,)), dma((12,)), dma((16,)), dma((2, 8)), dma((2, 8)), dma((2, 12)), dma((2, 16)),
            dma((2, 4)), dma((2, 8)), dma((2, 8)), dma((2, 8)), dma((2, 8)),
            dma((2, 2)), dma((2, 2)), dma((4, 4)), dma((4, 4)), dma((8, 8)), dma((8,)),
        ],
        compiler_params=pltpu.CompilerParams(
            has_side_effects=True, collective_id=1, vmem_limit_bytes=60 * 2**20
        ),
        name="levels",
    )(surface, refl, tiles, blocks, counts, pool)


def per_device(surface, refl, pool, tile_ids, block_ids, counts):
    image = run(surface, refl.reshape(8, 128), tile_ids[0], block_ids[0], counts, pool)
    return (image / 768.0).reshape(1, 1024)


def solution(mesh):
    placed = (
        P("freq", None, None, "lat"),
        P("depth", "lat"),
        P("depth", "freq", None, None, None),
        P("depth", "lat", None),
        P("depth", "lat", None),
        P("depth", "lat"),
    )
    return jax.shard_map(
        per_device, mesh=mesh, in_specs=placed, out_specs=P("depth", "lat"), check_vma=False
    )
```

```python
import jax
import jax.numpy as jnp
from jax import lax
from jax.experimental import pallas as pl
from jax.experimental.pallas import tpu as pltpu
from jax.sharding import PartitionSpec as P

MESH = pl.DeviceIdType.MESH
ANY = pl.BlockSpec(memory_space=pl.ANY)
VMEM = pl.BlockSpec(memory_space=pltpu.VMEM)
BF = jnp.bfloat16
F32 = jnp.float32
WIDE = 144
DEAD = 8 * WIDE


def remote(src, dst, send, recv, d, z, x, c):
    return pltpu.make_async_remote_copy(
        src_ref=src,
        dst_ref=dst,
        send_sem=send,
        recv_sem=recv,
        device_id=(d, z * 4 + x, c),
        device_id_type=MESH,
    )


def arrival(ref, sem):
    return pltpu.make_async_copy(ref, ref, sem)


def turned(rows):
    count = rows.shape[0]
    even = lax.broadcasted_iota(jnp.int32, rows.shape, 0) % 2 == 0
    return jnp.where(even, -pltpu.roll(rows, count - 1, 0), pltpu.roll(rows, 1, 0))


def kernel(
    surface, refl, tiles, blocks, counts, pool, out,
    raw, mixed, wsrc, draft, fac_y, ints_y, wave, field, pool_all, fac_all, ints_all, lists, prod, img, in_x, x_sum, in_yz, done, got,
    l_sem, w_send, w_recv, y_send, y_recv, m_send, m_recv,
    p_send, p_recv, q_send, q_recv, h_send, h_recv, i_send, i_recv, o_send, o_recv, e_sem,
):
    d = lax.axis_index("depth")
    a = lax.axis_index("lat")
    c = lax.axis_index("freq")
    z, x = a // 4, a % 4
    other = 1 - c
    active = z < 6
    side = z // 4
    near = side == c
    source = z // 3
    gives = jnp.logical_and(active, c == source)
    takes = jnp.logical_and(active, c != source)

    def wave_out(i):
        return 3 * c + i // 4, i % 4, side

    def wave_in(i):
        return 4 * c + i // 4, i % 4, source

    def is_me(tz, tx, tc):
        return jnp.logical_and(tz * 4 + tx == a, tc == c)

    def wave_copy(i):
        tz, tx, tc = wave_out(i)
        return remote(
            wsrc.at[i // 4, i % 4], wave.at[a % 16], w_send.at[i], w_recv.at[a % 16], d, tz, tx, tc
        )

    slot = x * 4 + z % 4

    def y_copies(step):
        to = (d + step) % 8
        return (
            remote(fac_y.at[d], fac_y.at[d], y_send.at[0, step], y_recv.at[0, step], to, z, x, c),
            remote(ints_y.at[d], ints_y.at[d], y_send.at[1, step], y_recv.at[1, step], to, z, x, c),
        )

    def list_copies(i):
        tz, tx, tc = wave_out(i)
        return [
            remote(column, whole.at[:, slot], m_send.at[kind, i], m_recv.at[kind, slot], d, tz, tx, tc)
            for kind, column, whole in ((0, fac_y, fac_all), (1, ints_y, ints_all))
        ]

    mine = pool.at[0, z % 3]

    def ring_copy(way, step, part):
        if way == 0:
            level, to = (d - step + 8) % 8, (d + 1) % 8
        else:
            level, to = (d + step) % 8, (d + 7) % 8
        at = pool_all.at[level, pl.ds(4 * c + 2 * part, 2)]
        i = 2 * step + part
        return remote(at, at, p_send.at[way, i], p_recv.at[way, i], to, z, x, c)

    def share(way, step, part):
        level = (d - 1 - step + 8) % 8 if way == 0 else (d + 1 + step) % 8
        at = pool_all.at[level, pl.ds(4 * c + 2 * part, 2)]
        i = 2 * step + part
        return remote(at, at, q_send.at[way, i], q_recv.at[way, i], d, z, x, other)

    ring = [(way, step, part) for step in range(3) for part in range(2) for way in range(2)]
    ring += [(0, 3, 0), (1, 3, 1)]

    here = pltpu.make_async_copy(mine, pool_all.at[d], l_sem.at[0])

    def over(k):
        blocks_here = pl.ds(4 * other if k == 0 else 4 * c, 4)
        return remote(
            mine.at[blocks_here], pool_all.at[d, blocks_here],
            l_sem.at[3 + k], l_sem.at[6 + k], d, z, x, other,
        )

    def came_over(k):
        return arrival(pool_all.at[d, pl.ds(4 * c if k == 0 else 4 * other, 4)], l_sem.at[6 + k])

    def edges(way, parity):
        own, theirs = ((64, 1088), (1024, 0))[way]
        return remote(
            field.at[parity, pl.ds(own, 64)], field.at[parity, pl.ds(theirs, 64)],
            h_send.at[parity, way], h_recv.at[parity, way], d, z, x, other,
        )

    barrier = pltpu.get_barrier_semaphore()

    def greet(d, z, x, c):
        pl.semaphore_signal(barrier, inc=1, device_id=(d, z * 4 + x, c), device_id_type=MESH)

    greet(d, z, x, other)
    for i in range(1, 8):
        greet((d + i) % 8, z, x, c)
    for i in range(1, 4):
        greet(d, z, (x + i) % 4, c)

    @pl.loop(0, 12)
    def _(i):
        @pl.when(jnp.logical_not(is_me(*wave_out(i))))
        def _():
            greet(d, *wave_out(i))

    @pl.when(active)
    def _():
        @pl.loop(0, 16)
        def _(i):
            @pl.when(jnp.logical_not(is_me(*wave_in(i))))
            def _():
                greet(d, *wave_in(i))

    loops = jnp.logical_and(gives, near).astype(jnp.int32)
    fetch = pltpu.make_async_copy(surface.at[:, :, pl.ds(16 * d, 16), :], raw, l_sem.at[5])
    fetch.start()

    @pl.when(gives)
    def _():
        here.start()

    lane = lax.broadcasted_iota(jnp.int32, (1, 128), 1)
    draft[...] = jnp.zeros((8, 128), jnp.int32)
    draft[:, :10] = 8 * (blocks[...] * WIDE + (tiles[...] - 128 * side + 8) % 256)
    line = jnp.zeros((1, 128), jnp.int32)
    for r in range(8):
        live = counts[0, r]
        fac_y[d, r : r + 1, :] = (1.0 - refl[r : r + 1, :]) * (
            1.0 / jnp.sqrt(jnp.full((1, 128), live, jnp.int32).astype(F32))
        )
        slots = jnp.where(lane < live, draft[r : r + 1, :], 8 * DEAD)
        slots = jnp.where(lane < 10, slots, 0)
        line = line + (slots if r == 0 else pltpu.roll(slots, 10 * r, 1))
    ints_y[d] = line

    fetch.wait()

    @pl.loop(0, 3)
    def _(f):
        for part in range(2):
            rows = raw[f, part].astype(F32)
            for tx in range(4):
                for t in range(8):
                    at = pl.ds(256 * f + 64 * tx + 8 * t + part, 4, stride=2)
                    mixed[at, :] = rows[4 * tx : 4 * tx + 4, 128 * t : 128 * t + 128]
        for tx in range(4):
            at = pl.ds(pl.multiple_of(256 * f + 64 * tx, 64), 64)
            wsrc[f, tx] = mixed[at, :].astype(BF)

    pl.semaphore_wait(barrier, 11 + 12 - loops + jnp.where(active, 16 - loops, 0))

    @pl.when(gives)
    def _():
        over(0).start()
        over(1).start()
        here.wait()

    @pl.when(takes)
    def _():
        came_over(0).wait()

    @pl.when(active)
    def _():
        for part in range(2):
            for way in range(2):
                ring_copy(way, 0, part).start()

    for step in range(1, 8):
        for copy in y_copies(step):
            copy.start()

    @pl.loop(0, 12)
    def _(i):
        same = is_me(*wave_out(i))

        @pl.when(same)
        def _():
            pltpu.make_async_copy(wsrc.at[i // 4, i % 4], wave.at[a % 16], l_sem.at[1]).start()

        @pl.when(jnp.logical_not(same))
        def _():
            wave_copy(i).start()

    for step in range(1, 8):
        for copy in y_copies(step):
            copy.wait_recv()

    @pl.loop(0, 12)
    def _(i):
        @pl.when(jnp.logical_not(is_me(*wave_out(i))))
        def _():
            for copy in list_copies(i):
                copy.start()

    @pl.when(jnp.logical_and(gives, near))
    def _():
        fac_all[:, slot] = fac_y[...]
        ints_all[:, slot] = ints_y[...]

    def ring_steps(these):
        for way, step, part in these:
            ring_copy(way, step, part).wait_recv()
            if (way, step + 1, part) in ring:
                ring_copy(way, step + 1, part).start()
            share(way, step, part).start()

    @pl.when(active)
    def _():
        ring_steps(ring[:4])

        @pl.loop(0, 16)
        def _(i):
            same = is_me(*wave_in(i))

            @pl.when(same)
            def _():
                arrival(wave.at[i], l_sem.at[1]).wait()

            @pl.when(jnp.logical_not(same))
            def _():
                arrival(wave.at[i], w_recv.at[i]).wait()

            at = pl.ds(pl.multiple_of(64 + 64 * i, 64), 64)
            rows = wave[i]
            field[0, at, :128] = rows
            field[0, at, 128:] = turned(rows.astype(F32)).astype(BF)

        edges(0, 0).start()
        edges(1, 0).start()
        prod[pl.ds(8 * DEAD, 8), :] = jnp.zeros((8, 128), F32)
        ring_steps(ring[4:12])

        @pl.loop(0, 16)
        def _(i):
            @pl.when(jnp.logical_not(is_me(*wave_in(i))))
            def _():
                at = (i % 4) * 4 + i // 4
                arrival(fac_all.at[:, at], m_recv.at[0, at]).wait()
                arrival(ints_all.at[:, at], m_recv.at[1, at]).wait()

        to_scalars = pltpu.make_async_copy(ints_all, lists, l_sem.at[2])
        to_scalars.start()
        ring_steps(ring[12:])
        to_scalars.wait()

        @pl.when(takes)
        def _():
            came_over(1).wait()

        for copy in ring:
            share(*copy).wait_recv()

        batches = ((0, 5), (5, 2), (7, 1))

        def image_copy(batch, step):
            first, count = batches[batch]
            to = (x + step) % 4
            return remote(
                img.at[pl.ds(first, count), pl.ds(4 * to, 4)], in_x.at[step, pl.ds(first, count)],
                i_send.at[batch, step], i_recv.at[batch, step], d, z, to, c,
            )

        def owner_copy(level, k):
            return remote(
                x_sum.at[level, k], in_yz.at[d, z], o_send.at[level, k], o_recv.at[d],
                level, 4 * c + k, x, c,
            )

        def is_owner(level, k):
            return jnp.logical_and(level == d, 4 * c + k == z)

        def send_images(batch):
            for step in range(1, 4):
                image_copy(batch, step).start()

        def hand_in(batch):
            for step in range(1, 4):
                image_copy(batch, step).wait_recv()

            @pl.loop(batches[batch][0], sum(batches[batch]))
            def _(level):
                x_sum[level] = (img[level, pl.ds(4 * x, 4)] + in_x[1, level]) + (
                    in_x[2, level] + in_x[3, level]
                )
                for k in range(4):
                    @pl.when(is_owner(level, k))
                    def _():
                        in_yz[d, z] = x_sum[level, k]

                    @pl.when(jnp.logical_not(is_owner(level, k)))
                    def _():
                        owner_copy(level, k).start()

        def group(level, now, g):
            later = 1 - now
            for m in range(16):
                new = []
                for r in (2 * m, 2 * m + 1):
                    block = 4 * g + r // 8
                    at = (block % 4) * 4 + block // 4
                    parts = []
                    for k in range(10):
                        parts.append(prod[pl.ds(lists[level, at, 0, r % 8 * 10 + k], 8), :])
                    while len(parts) > 1:
                        parts = [sum(parts[i + 1 : i + 2], parts[i]) for i in range(0, len(parts), 2)]
                    row = parts[0] * fac_all[level, at, r % 8 : r % 8 + 1, :]
                    img[level, at, r % 8 : r % 8 + 1, :] = jnp.sum(row * row, axis=0, keepdims=True)
                    new.append(row)
                pair = jnp.concatenate(new, 0)
                at = pl.ds(pl.multiple_of(64 + 256 * g + 16 * m, 16), 16)
                field[later, at, :128] = pair.astype(BF)
                field[later, at, 128:] = turned(pair).astype(BF)

        @pl.loop(0, 8)
        def _(level):
            now = level % 2
            for way in range(2):
                edges(way, now).wait()
            for p in range(4):
                b0, b1 = pool_all[level, 2 * p], pool_all[level, 2 * p + 1]
                weights = jnp.concatenate(
                    [
                        jnp.concatenate([b0[:, :128], b1[:, :128]], 1),
                        jnp.concatenate([b0[:, 128:], b1[:, 128:]], 1),
                    ],
                    0,
                )
                product = jnp.dot(field[now], weights, preferred_element_type=F32)
                for k in range(2):
                    rows = pl.ds((2 * p + k) * 8 * WIDE, 8 * WIDE)
                    prod[rows, :] = product[:, 128 * k : 128 * k + 128]

            @pl.loop(0, 2)
            def _(i):
                group(level, now, 3 * i)

            @pl.when(level < 7)
            def _():
                for way in range(2):
                    edges(way, 1 - now).start()

            @pl.loop(1, 3)
            def _(g):
                group(level, now, g)

            for batch in range(3):
                @pl.when(level == sum(batches[batch]) - 1)
                def _():
                    send_images(batch)

        for batch in range(3):
            hand_in(batch)

        for batch in range(3):
            for step in range(1, 4):
                image_copy(batch, step).wait_send()

        @pl.loop(0, 8)
        def _(level):
            for k in range(4):
                @pl.when(jnp.logical_not(is_owner(level, k)))
                def _():
                    owner_copy(level, k).wait_send()

    echo = remote(done, got, e_sem.at[0], e_sem.at[1], d, z, x, other)

    @pl.when(near)
    def _():
        total = jnp.zeros((8, 128), F32)
        for fd in range(8):
            local = jnp.logical_and(active, d == fd)

            @pl.when(local)
            def _():
                arrival(in_yz.at[fd, pl.ds(0, 5)], o_recv.at[fd]).wait()

            @pl.when(jnp.logical_not(local))
            def _():
                arrival(in_yz.at[fd, pl.ds(0, 6)], o_recv.at[fd]).wait()

        for fd in range(8):
            for fz in range(6):
                total = total + in_yz[fd, fz]
        done[...] = total
        echo.start()
        out[...] = total
        echo.wait_send()

    @pl.when(jnp.logical_not(near))
    def _():
        echo.wait_recv()
        out[...] = got[...]

    for step in range(1, 8):
        for copy in y_copies(step):
            copy.wait_send()

    @pl.loop(0, 12)
    def _(i):
        @pl.when(jnp.logical_not(is_me(*wave_out(i))))
        def _():
            wave_copy(i).wait_send()
            for copy in list_copies(i):
                copy.wait_send()

    @pl.when(gives)
    def _():
        over(0).wait_send()
        over(1).wait_send()

    @pl.when(active)
    def _():
        for way, step, part in ring:
            ring_copy(way, step, part).wait_send()
            share(way, step, part).wait_send()


def run(surface, refl, tiles, blocks, counts, pool):
    dma = pltpu.SemaphoreType.DMA
    vmem = pltpu.VMEM
    return pl.pallas_call(
        kernel,
        out_shape=jax.ShapeDtypeStruct((8, 128), F32),
        in_specs=[ANY, VMEM, VMEM, VMEM, pl.BlockSpec(memory_space=pltpu.SMEM), ANY],
        out_specs=VMEM,
        scratch_shapes=[
            vmem((3, 2, 16, 1024), BF),
            vmem((768, 128), F32),
            vmem((3, 4, 64, 128), BF),
            vmem((8, 128), jnp.int32),
            vmem((8, 8, 128), F32),
            vmem((8, 1, 128), jnp.int32),
            vmem((16, 64, 128), BF),
            vmem((2, 8 * WIDE, 256), BF),
            vmem((8, 8, 128, 256), BF),
            vmem((8, 16, 8, 128), F32),
            vmem((8, 16, 1, 128), jnp.int32),
            pltpu.SMEM((8, 16, 1, 128), jnp.int32),
            vmem((8 * DEAD + 8, 128), F32),
            vmem((8, 16, 8, 128), F32),
            vmem((4, 8, 4, 8, 128), F32),
            vmem((8, 4, 8, 128), F32),
            vmem((8, 8, 8, 128), F32),
            vmem((8, 128), F32),
            vmem((8, 128), F32),
            dma((8,)), dma((12,)), dma((16,)), dma((2, 8)), dma((2, 8)), dma((2, 12)), dma((2, 16)),
            dma((2, 8)), dma((2, 8)), dma((2, 8)), dma((2, 8)),
            dma((2, 2)), dma((2, 2)), dma((3, 4)), dma((3, 4)), dma((8, 4)), dma((8,)), dma((2,)),
        ],
        compiler_params=pltpu.CompilerParams(
            has_side_effects=True, collective_id=1, vmem_limit_bytes=60 * 2**20
        ),
        name="levels",
    )(surface, refl, tiles, blocks, counts, pool)


def per_device(surface, refl, pool, tile_ids, block_ids, counts):
    image = run(surface, refl.reshape(8, 128), tile_ids[0], block_ids[0], counts, pool)
    return (image / 768.0).reshape(1, 1024)


def solution(mesh):
    placed = (
        P("freq", None, None, "lat"),
        P("depth", "lat"),
        P("depth", "freq", None, None, None),
        P("depth", "lat", None),
        P("depth", "lat", None),
        P("depth", "lat"),
    )
    return jax.shard_map(
        per_device, mesh=mesh, in_specs=placed, out_specs=P("depth", "lat"), check_vma=False
    )
```

```python
import jax
import jax.numpy as jnp
from jax import lax
from jax.experimental import pallas as pl
from jax.experimental.pallas import tpu as pltpu
from jax.sharding import PartitionSpec as P

MESH = pl.DeviceIdType.MESH
ANY = pl.BlockSpec(memory_space=pl.ANY)
VMEM = pl.BlockSpec(memory_space=pltpu.VMEM)
BF = jnp.bfloat16
F32 = jnp.float32
WIDE = 144
DEAD = 8 * WIDE


def remote(src, dst, send, recv, d, z, x, c):
    return pltpu.make_async_remote_copy(
        src_ref=src,
        dst_ref=dst,
        send_sem=send,
        recv_sem=recv,
        device_id=(d, z * 4 + x, c),
        device_id_type=MESH,
    )


def arrival(ref, sem):
    return pltpu.make_async_copy(ref, ref, sem)


def turned(rows):
    count = rows.shape[0]
    even = lax.broadcasted_iota(jnp.int32, rows.shape, 0) % 2 == 0
    return jnp.where(even, -pltpu.roll(rows, count - 1, 0), pltpu.roll(rows, 1, 0))


def kernel(
    surface, refl, tiles, blocks, counts, pool, out,
    raw, mixed, wsrc, draft, fac_y, ints_y, wave, field, pool_all, fac_all, ints_all, lists, prod, img, in_x, x_sum, in_yz, done, got,
    l_sem, w_send, w_recv, y_send, y_recv, m_send, m_recv,
    p_send, p_recv, q_send, q_recv, g_send, g_recv, t_send, t_recv, h_send, h_recv, i_send, i_recv, o_send, o_recv, e_sem,
):
    d = lax.axis_index("depth")
    a = lax.axis_index("lat")
    c = lax.axis_index("freq")
    z, x = a // 4, a % 4
    other = 1 - c
    active = z < 6
    side = z // 4
    near = side == c
    source = z // 3
    gives = jnp.logical_and(active, c == source)
    takes = jnp.logical_and(active, c != source)

    def wave_out(i):
        return 3 * c + i // 4, i % 4, side

    def wave_in(i):
        return 4 * c + i // 4, i % 4, source

    def is_me(tz, tx, tc):
        return jnp.logical_and(tz * 4 + tx == a, tc == c)

    def wave_copy(i):
        tz, tx, tc = wave_out(i)
        return remote(
            wsrc.at[i // 4, i % 4], wave.at[a % 16], w_send.at[i], w_recv.at[a % 16], d, tz, tx, tc
        )

    slot = x * 4 + z % 4

    def y_copies(step):
        to = (d + step) % 8
        return (
            remote(fac_y.at[d], fac_y.at[d], y_send.at[0, step], y_recv.at[0, step], to, z, x, c),
            remote(ints_y.at[d], ints_y.at[d], y_send.at[1, step], y_recv.at[1, step], to, z, x, c),
        )

    def list_copies(i):
        tz, tx, tc = wave_out(i)
        soon, late = pl.ds(0, 2), pl.ds(2, 6)
        return [
            remote(column, target, m_send.at[kind, i], m_recv.at[kind, slot], d, tz, tx, tc)
            for kind, (column, target) in enumerate(
                (
                    (fac_y.at[soon], fac_all.at[soon, slot]),
                    (ints_y, ints_all.at[:, slot]),
                    (fac_y.at[late], fac_all.at[late, slot]),
                )
            )
        ]

    mine = pool.at[0, z % 3]
    unit = x % 2 * 2 + c
    across = (x + 1) % 2 * 2 + c

    def ring_copy(way, step, part):
        if way == 0:
            level, to = (d - step + 8) % 8, (d + 1) % 8
        else:
            level, to = (d + step) % 8, (d + 7) % 8
        at = pool_all.at[level, pl.ds(2 * unit + part, 1)]
        i = 2 * step + part
        return remote(at, at, p_send.at[way, i], p_recv.at[way, i], to, z, x, c)

    def came(way, step):
        return (d - 1 - step + 8) % 8 if way == 0 else (d + 1 + step) % 8

    def share(way, step, part):
        at = pool_all.at[came(way, step), pl.ds(2 * unit + part, 1)]
        i = 2 * step + part
        return remote(at, at, q_send.at[way, i], q_recv.at[way, i], d, z, x, other)

    def cross(way, step, part):
        at = pool_all.at[came(way, step), pl.ds(2 * unit + part, 1)]
        i, to = 2 * step + part, (x + 1 + 2 * part) % 4
        return remote(at, at, g_send.at[way, i], g_recv.at[way, i], d, z, to, c)

    def pass_on(way, step, part):
        at = pool_all.at[came(way, step), pl.ds(2 * across + part, 1)]
        i = 2 * step + part
        return arrival(at, g_recv.at[way, i]), remote(
            at, at, t_send.at[way, i], t_recv.at[way, i], d, z, x, other
        )

    ring = [(way, step, part) for step in range(3) for part in range(2) for way in range(2)]
    ring += [(0, 3, 0), (1, 3, 1)]

    here = pltpu.make_async_copy(mine, pool_all.at[d], l_sem.at[0])

    def over(k):
        blocks_here = pl.ds(4 * ((x + k) % 2), 4)
        return remote(
            mine.at[blocks_here], pool_all.at[d, blocks_here],
            l_sem.at[3 + k], l_sem.at[6 + k], d, z, x, other,
        )

    def came_over(k):
        return arrival(pool_all.at[d, pl.ds(4 * ((x + k) % 2), 4)], l_sem.at[6 + k])

    def edges(way, parity):
        own, theirs = ((64, 1088), (1024, 0))[way]
        return remote(
            field.at[parity, pl.ds(own, 64)], field.at[parity, pl.ds(theirs, 64)],
            h_send.at[parity, way], h_recv.at[parity, way], d, z, x, other,
        )

    barrier = pltpu.get_barrier_semaphore()

    def greet(d, z, x, c):
        pl.semaphore_signal(barrier, inc=1, device_id=(d, z * 4 + x, c), device_id_type=MESH)

    greet(d, z, x, other)
    for i in range(1, 8):
        greet((d + i) % 8, z, x, c)
    for i in range(1, 4):
        greet(d, z, (x + i) % 4, c)

    @pl.loop(0, 12)
    def _(i):
        @pl.when(jnp.logical_not(is_me(*wave_out(i))))
        def _():
            greet(d, *wave_out(i))

    @pl.when(active)
    def _():
        @pl.loop(0, 16)
        def _(i):
            @pl.when(jnp.logical_not(is_me(*wave_in(i))))
            def _():
                greet(d, *wave_in(i))

    loops = jnp.logical_and(gives, near).astype(jnp.int32)
    fetch = pltpu.make_async_copy(surface.at[:, :, pl.ds(16 * d, 16), :], raw, l_sem.at[5])
    fetch.start()

    @pl.when(gives)
    def _():
        here.start()

    lane = lax.broadcasted_iota(jnp.int32, (1, 128), 1)
    draft[...] = jnp.zeros((8, 128), jnp.int32)
    draft[:, :10] = 8 * (blocks[...] * WIDE + (tiles[...] - 128 * side + 8) % 256)
    line = jnp.zeros((1, 128), jnp.int32)
    for r in range(8):
        live = counts[0, r]
        fac_y[d, r : r + 1, :] = (1.0 - refl[r : r + 1, :]) * (
            1.0 / jnp.sqrt(jnp.full((1, 128), live, jnp.int32).astype(F32))
        )
        slots = jnp.where(lane < live, draft[r : r + 1, :], 8 * DEAD)
        slots = jnp.where(lane < 10, slots, 0)
        line = line + (slots if r == 0 else pltpu.roll(slots, 10 * r, 1))
    ints_y[d] = line

    fetch.wait()

    @pl.loop(0, 3)
    def _(f):
        for part in range(2):
            rows = raw[f, part].astype(F32)
            for tx in range(4):
                for t in range(8):
                    at = pl.ds(256 * f + 64 * tx + 8 * t + part, 4, stride=2)
                    mixed[at, :] = rows[4 * tx : 4 * tx + 4, 128 * t : 128 * t + 128]
        for tx in range(4):
            at = pl.ds(pl.multiple_of(256 * f + 64 * tx, 64), 64)
            wsrc[f, tx] = mixed[at, :].astype(BF)

    pl.semaphore_wait(barrier, 11 + 12 - loops + jnp.where(active, 16 - loops, 0))

    @pl.when(gives)
    def _():
        over(0).start()
        over(1).start()
        here.wait()

    @pl.when(takes)
    def _():
        came_over(0).wait()

    @pl.when(active)
    def _():
        for part in range(2):
            for way in range(2):
                ring_copy(way, 0, part).start()

    for step in range(1, 8):
        for copy in y_copies(step):
            copy.start()

    @pl.loop(0, 12)
    def _(i):
        same = is_me(*wave_out(i))

        @pl.when(same)
        def _():
            pltpu.make_async_copy(wsrc.at[i // 4, i % 4], wave.at[a % 16], l_sem.at[1]).start()

        @pl.when(jnp.logical_not(same))
        def _():
            wave_copy(i).start()

    for step in range(1, 8):
        for copy in y_copies(step):
            copy.wait_recv()

    @pl.loop(0, 12)
    def _(i):
        @pl.when(jnp.logical_not(is_me(*wave_out(i))))
        def _():
            for copy in list_copies(i)[:2]:
                copy.start()

    @pl.loop(0, 12)
    def _(i):
        @pl.when(jnp.logical_not(is_me(*wave_out(i))))
        def _():
            list_copies(i)[2].start()

    @pl.when(jnp.logical_and(gives, near))
    def _():
        fac_all[:, slot] = fac_y[...]
        ints_all[:, slot] = ints_y[...]

    def ring_steps(these):
        for way, step, part in these:
            ring_copy(way, step, part).wait_recv()
            if (way, step + 1, part) in ring:
                ring_copy(way, step + 1, part).start()
            cross(way, step, part).start()
            share(way, step, part).start()

    def cross_steps(these):
        for copy in these:
            came_across, onward = pass_on(*copy)
            came_across.wait()
            onward.start()

    @pl.when(active)
    def _():
        ring_steps(ring[:4])

        @pl.loop(0, 16)
        def _(i):
            same = is_me(*wave_in(i))

            @pl.when(same)
            def _():
                arrival(wave.at[i], l_sem.at[1]).wait()

            @pl.when(jnp.logical_not(same))
            def _():
                arrival(wave.at[i], w_recv.at[i]).wait()

            at = pl.ds(pl.multiple_of(64 + 64 * i, 64), 64)
            rows = wave[i]
            field[0, at, :128] = rows
            field[0, at, 128:] = turned(rows.astype(F32)).astype(BF)

        edges(0, 0).start()
        edges(1, 0).start()
        prod[pl.ds(8 * DEAD, 8), :] = jnp.zeros((8, 128), F32)
        ring_steps(ring[4:8])
        cross_steps(ring[:4])
        ring_steps(ring[8:12])
        cross_steps(ring[4:8])

        @pl.loop(0, 16)
        def _(i):
            @pl.when(jnp.logical_not(is_me(*wave_in(i))))
            def _():
                at = (i % 4) * 4 + i // 4
                arrival(fac_all.at[pl.ds(0, 2), at], m_recv.at[0, at]).wait()
                arrival(ints_all.at[:, at], m_recv.at[1, at]).wait()

        to_scalars = pltpu.make_async_copy(ints_all, lists, l_sem.at[2])
        to_scalars.start()
        ring_steps(ring[12:])
        cross_steps(ring[8:])
        to_scalars.wait()

        @pl.when(takes)
        def _():
            came_over(1).wait()

        for copy in ring:
            share(*copy).wait_recv()
            pass_on(*copy)[1].wait_recv()

        batches = ((0, 5), (5, 2), (7, 1))

        def image_copy(batch, step):
            first, count = batches[batch]
            to = (x + step) % 4
            return remote(
                img.at[pl.ds(first, count), pl.ds(4 * to, 4)], in_x.at[step, pl.ds(first, count)],
                i_send.at[batch, step], i_recv.at[batch, step], d, z, to, c,
            )

        def owner_copy(level, k):
            return remote(
                x_sum.at[level, k], in_yz.at[d, z], o_send.at[level, k], o_recv.at[d],
                level, 4 * c + k, x, c,
            )

        def is_owner(level, k):
            return jnp.logical_and(level == d, 4 * c + k == z)

        def send_images(batch):
            for step in range(1, 4):
                image_copy(batch, step).start()

        def hand_in(batch):
            for step in range(1, 4):
                image_copy(batch, step).wait_recv()

            @pl.loop(batches[batch][0], sum(batches[batch]))
            def _(level):
                x_sum[level] = (img[level, pl.ds(4 * x, 4)] + in_x[1, level]) + (
                    in_x[2, level] + in_x[3, level]
                )
                for k in range(4):
                    @pl.when(is_owner(level, k))
                    def _():
                        in_yz[d, z] = x_sum[level, k]

                    @pl.when(jnp.logical_not(is_owner(level, k)))
                    def _():
                        owner_copy(level, k).start()

        def group(level, now, g):
            later = 1 - now
            for m in range(16):
                new = []
                for r in (2 * m, 2 * m + 1):
                    block = 4 * g + r // 8
                    at = (block % 4) * 4 + block // 4
                    parts = []
                    for k in range(10):
                        parts.append(prod[pl.ds(lists[level, at, 0, r % 8 * 10 + k], 8), :])
                    while len(parts) > 1:
                        parts = [sum(parts[i + 1 : i + 2], parts[i]) for i in range(0, len(parts), 2)]
                    row = parts[0] * fac_all[level, at, r % 8 : r % 8 + 1, :]
                    img[level, at, r % 8 : r % 8 + 1, :] = jnp.sum(row * row, axis=0, keepdims=True)
                    new.append(row)
                pair = jnp.concatenate(new, 0)
                at = pl.ds(pl.multiple_of(64 + 256 * g + 16 * m, 16), 16)
                field[later, at, :128] = pair.astype(BF)
                field[later, at, 128:] = turned(pair).astype(BF)

        @pl.loop(0, 8)
        def _(level):
            now = level % 2

            @pl.when(level == 2)
            def _():
                @pl.loop(0, 16)
                def _(i):
                    @pl.when(jnp.logical_not(is_me(*wave_in(i))))
                    def _():
                        at = (i % 4) * 4 + i // 4
                        arrival(fac_all.at[pl.ds(2, 6), at], m_recv.at[2, at]).wait()

            for way in range(2):
                edges(way, now).wait()
            for p in range(4):
                b0, b1 = pool_all[level, 2 * p], pool_all[level, 2 * p + 1]
                weights = jnp.concatenate(
                    [
                        jnp.concatenate([b0[:, :128], b1[:, :128]], 1),
                        jnp.concatenate([b0[:, 128:], b1[:, 128:]], 1),
                    ],
                    0,
                )
                product = jnp.dot(field[now], weights, preferred_element_type=F32)
                for k in range(2):
                    rows = pl.ds((2 * p + k) * 8 * WIDE, 8 * WIDE)
                    prod[rows, :] = product[:, 128 * k : 128 * k + 128]

            @pl.loop(0, 2)
            def _(i):
                group(level, now, 3 * i)

            @pl.when(level < 7)
            def _():
                for way in range(2):
                    edges(way, 1 - now).start()

            @pl.loop(1, 3)
            def _(g):
                group(level, now, g)

            for batch in range(3):
                @pl.when(level == sum(batches[batch]) - 1)
                def _():
                    send_images(batch)

        for batch in range(3):
            hand_in(batch)

        for batch in range(3):
            for step in range(1, 4):
                image_copy(batch, step).wait_send()

        @pl.loop(0, 8)
        def _(level):
            for k in range(4):
                @pl.when(jnp.logical_not(is_owner(level, k)))
                def _():
                    owner_copy(level, k).wait_send()

    echo = remote(done, got, e_sem.at[0], e_sem.at[1], d, z, x, other)

    @pl.when(near)
    def _():
        total = jnp.zeros((8, 128), F32)
        for fd in range(8):
            local = jnp.logical_and(active, d == fd)

            @pl.when(local)
            def _():
                arrival(in_yz.at[fd, pl.ds(0, 5)], o_recv.at[fd]).wait()

            @pl.when(jnp.logical_not(local))
            def _():
                arrival(in_yz.at[fd, pl.ds(0, 6)], o_recv.at[fd]).wait()

        for fd in range(8):
            for fz in range(6):
                total = total + in_yz[fd, fz]
        done[...] = total
        echo.start()
        out[...] = total
        echo.wait_send()

    @pl.when(jnp.logical_not(near))
    def _():
        echo.wait_recv()
        out[...] = got[...]

    for step in range(1, 8):
        for copy in y_copies(step):
            copy.wait_send()

    @pl.loop(0, 12)
    def _(i):
        @pl.when(jnp.logical_not(is_me(*wave_out(i))))
        def _():
            wave_copy(i).wait_send()
            for copy in list_copies(i):
                copy.wait_send()

    @pl.when(gives)
    def _():
        over(0).wait_send()
        over(1).wait_send()

    @pl.when(active)
    def _():
        for way, step, part in ring:
            ring_copy(way, step, part).wait_send()
            share(way, step, part).wait_send()
            cross(way, step, part).wait_send()
            pass_on(way, step, part)[1].wait_send()


def run(surface, refl, tiles, blocks, counts, pool):
    dma = pltpu.SemaphoreType.DMA
    vmem = pltpu.VMEM
    return pl.pallas_call(
        kernel,
        out_shape=jax.ShapeDtypeStruct((8, 128), F32),
        in_specs=[ANY, VMEM, VMEM, VMEM, pl.BlockSpec(memory_space=pltpu.SMEM), ANY],
        out_specs=VMEM,
        scratch_shapes=[
            vmem((3, 2, 16, 1024), BF),
            vmem((768, 128), F32),
            vmem((3, 4, 64, 128), BF),
            vmem((8, 128), jnp.int32),
            vmem((8, 8, 128), F32),
            vmem((8, 1, 128), jnp.int32),
            vmem((16, 64, 128), BF),
            vmem((2, 8 * WIDE, 256), BF),
            vmem((8, 8, 128, 256), BF),
            vmem((8, 16, 8, 128), F32),
            vmem((8, 16, 1, 128), jnp.int32),
            pltpu.SMEM((8, 16, 1, 128), jnp.int32),
            vmem((8 * DEAD + 8, 128), F32),
            vmem((8, 16, 8, 128), F32),
            vmem((4, 8, 4, 8, 128), F32),
            vmem((8, 4, 8, 128), F32),
            vmem((8, 8, 8, 128), F32),
            vmem((8, 128), F32),
            vmem((8, 128), F32),
            dma((8,)), dma((12,)), dma((16,)), dma((2, 8)), dma((2, 8)), dma((3, 12)), dma((3, 16)),
            dma((2, 8)), dma((2, 8)), dma((2, 8)), dma((2, 8)),
            dma((2, 8)), dma((2, 8)), dma((2, 8)), dma((2, 8)),
            dma((2, 2)), dma((2, 2)), dma((3, 4)), dma((3, 4)), dma((8, 4)), dma((8,)), dma((2,)),
        ],
        compiler_params=pltpu.CompilerParams(
            has_side_effects=True, collective_id=1, vmem_limit_bytes=60 * 2**20
        ),
        name="levels",
    )(surface, refl, tiles, blocks, counts, pool)


def per_device(surface, refl, pool, tile_ids, block_ids, counts):
    image = run(surface, refl.reshape(8, 128), tile_ids[0], block_ids[0], counts, pool)
    return (image / 768.0).reshape(1, 1024)


def solution(mesh):
    placed = (
        P("freq", None, None, "lat"),
        P("depth", "lat"),
        P("depth", "freq", None, None, None),
        P("depth", "lat", None),
        P("depth", "lat", None),
        P("depth", "lat"),
    )
    return jax.shard_map(
        per_device, mesh=mesh, in_specs=placed, out_specs=P("depth", "lat"), check_vma=False
    )
```

```python
import jax
import jax.numpy as jnp
from jax import lax
from jax.experimental import pallas as pl
from jax.experimental.pallas import tpu as pltpu
from jax.sharding import PartitionSpec as P

MESH = pl.DeviceIdType.MESH
ANY = pl.BlockSpec(memory_space=pl.ANY)
VMEM = pl.BlockSpec(memory_space=pltpu.VMEM)
BF = jnp.bfloat16
F32 = jnp.float32
WIDE = 144
DEAD = 8 * WIDE


def remote(src, dst, send, recv, d, z, x, c):
    return pltpu.make_async_remote_copy(
        src_ref=src,
        dst_ref=dst,
        send_sem=send,
        recv_sem=recv,
        device_id=(d, z * 4 + x, c),
        device_id_type=MESH,
    )


def arrival(ref, sem):
    return pltpu.make_async_copy(ref, ref, sem)


def turned(rows):
    count = rows.shape[0]
    even = lax.broadcasted_iota(jnp.int32, rows.shape, 0) % 2 == 0
    return jnp.where(even, -pltpu.roll(rows, count - 1, 0), pltpu.roll(rows, 1, 0))


def kernel(
    surface, refl, tiles, blocks, counts, pool, out,
    raw, mixed, wsrc, draft, fac_y, ints_y, wave, field, pool_all, fac_all, ints_all, lists, prod, img, in_x, x_sum, in_yz, done, got,
    l_sem, w_send, w_recv, y_send, y_recv, m_send, m_recv,
    p_send, p_recv, q_send, q_recv, g_send, g_recv, t_send, t_recv, h_send, h_recv, i_send, i_recv, o_send, o_recv, e_sem,
):
    d = lax.axis_index("depth")
    a = lax.axis_index("lat")
    c = lax.axis_index("freq")
    z, x = a // 4, a % 4
    other = 1 - c
    active = z < 6
    side = z // 4
    near = side == c
    source = z // 3
    gives = jnp.logical_and(active, c == source)
    takes = jnp.logical_and(active, c != source)

    def wave_out(i):
        return 3 * c + i // 4, i % 4, side

    def wave_in(i):
        return 4 * c + i // 4, i % 4, source

    def is_me(tz, tx, tc):
        return jnp.logical_and(tz * 4 + tx == a, tc == c)

    def wave_copy(i):
        tz, tx, tc = wave_out(i)
        return remote(
            wsrc.at[i // 4, i % 4], wave.at[a % 16], w_send.at[i], w_recv.at[a % 16], d, tz, tx, tc
        )

    slot = x * 4 + z % 4

    def y_copies(step):
        to = (d + step) % 8
        return (
            remote(fac_y.at[d], fac_y.at[d], y_send.at[0, step], y_recv.at[0, step], to, z, x, c),
            remote(ints_y.at[d], ints_y.at[d], y_send.at[1, step], y_recv.at[1, step], to, z, x, c),
        )

    def list_copies(i):
        tz, tx, tc = wave_out(i)
        soon, late = pl.ds(0, 2), pl.ds(2, 6)
        return [
            remote(column, target, m_send.at[kind, i], m_recv.at[kind, slot], d, tz, tx, tc)
            for kind, (column, target) in enumerate(
                (
                    (fac_y.at[soon], fac_all.at[soon, slot]),
                    (ints_y, ints_all.at[:, slot]),
                    (fac_y.at[late], fac_all.at[late, slot]),
                )
            )
        ]

    mine = pool.at[0, z % 3]
    unit = x % 2 * 2 + c
    across = (x + 1) % 2 * 2 + c

    def ring_copy(way, step, part):
        if way == 0:
            level, to = (d - step + 8) % 8, (d + 1) % 8
        else:
            level, to = (d + step) % 8, (d + 7) % 8
        at = pool_all.at[level, pl.ds(2 * unit + part, 1)]
        i = 2 * step + part
        return remote(at, at, p_send.at[way, i], p_recv.at[way, i], to, z, x, c)

    def came(way, step):
        return (d - 1 - step + 8) % 8 if way == 0 else (d + 1 + step) % 8

    def both(first, step, part):
        return pl.ds(2 * first, 2) if step < 3 else pl.ds(2 * first + part, 1)

    def share(way, step, part):
        at = pool_all.at[came(way, step), both(unit, step, part)]
        i = 2 * step + part
        return remote(at, at, q_send.at[way, i], q_recv.at[way, i], d, z, x, other)

    def cross(way, step, part):
        at = pool_all.at[came(way, step), pl.ds(2 * unit + part, 1)]
        i, to = 2 * step + part, (x + 1 + 2 * part) % 4
        return remote(at, at, g_send.at[way, i], g_recv.at[way, i], d, z, to, c)

    def pass_on(way, step, part):
        at = pool_all.at[came(way, step), pl.ds(2 * across + part, 1)]
        pair = pool_all.at[came(way, step), both(across, step, part)]
        i = 2 * step + part
        return arrival(at, g_recv.at[way, i]), remote(
            pair, pair, t_send.at[way, i], t_recv.at[way, i], d, z, x, other
        )

    ring = [(way, step, part) for step in range(3) for part in range(2) for way in range(2)]
    ring += [(0, 3, 0), (1, 3, 1)]
    whole = [copy for copy in ring if copy[1] == 3 or copy[2] == 1]

    here = pltpu.make_async_copy(mine, pool_all.at[d], l_sem.at[0])

    def over(k):
        blocks_here = pl.ds(4 * ((x + k) % 2), 4)
        return remote(
            mine.at[blocks_here], pool_all.at[d, blocks_here],
            l_sem.at[3 + k], l_sem.at[6 + k], d, z, x, other,
        )

    def came_over(k):
        return arrival(pool_all.at[d, pl.ds(4 * ((x + k) % 2), 4)], l_sem.at[6 + k])

    def edges(way, parity):
        own, theirs = ((64, 1088), (1024, 0))[way]
        return remote(
            field.at[parity, pl.ds(own, 64)], field.at[parity, pl.ds(theirs, 64)],
            h_send.at[parity, way], h_recv.at[parity, way], d, z, x, other,
        )

    barrier = pltpu.get_barrier_semaphore()

    def greet(d, z, x, c):
        pl.semaphore_signal(barrier, inc=1, device_id=(d, z * 4 + x, c), device_id_type=MESH)

    greet(d, z, x, other)
    for i in range(1, 8):
        greet((d + i) % 8, z, x, c)
    for i in range(1, 4):
        greet(d, z, (x + i) % 4, c)

    @pl.loop(0, 12, unroll=True)
    def _(i):
        @pl.when(jnp.logical_not(is_me(*wave_out(i))))
        def _():
            greet(d, *wave_out(i))

    @pl.when(active)
    def _():
        @pl.loop(0, 16, unroll=True)
        def _(i):
            @pl.when(jnp.logical_not(is_me(*wave_in(i))))
            def _():
                greet(d, *wave_in(i))

    loops = jnp.logical_and(gives, near).astype(jnp.int32)
    fetch = pltpu.make_async_copy(surface.at[:, :, pl.ds(16 * d, 16), :], raw, l_sem.at[5])
    fetch.start()

    @pl.when(gives)
    def _():
        here.start()

    lane = lax.broadcasted_iota(jnp.int32, (1, 128), 1)
    draft[...] = jnp.zeros((8, 128), jnp.int32)
    draft[:, :10] = 8 * (blocks[...] * WIDE + (tiles[...] - 128 * side + 8) % 256)
    line = jnp.zeros((1, 128), jnp.int32)
    for r in range(8):
        live = counts[0, r]
        fac_y[d, r : r + 1, :] = (1.0 - refl[r : r + 1, :]) * (
            1.0 / jnp.sqrt(jnp.full((1, 128), live, jnp.int32).astype(F32))
        )
        slots = jnp.where(lane < live, draft[r : r + 1, :], 8 * DEAD)
        slots = jnp.where(lane < 10, slots, 0)
        line = line + (slots if r == 0 else pltpu.roll(slots, 10 * r, 1))
    ints_y[d] = line

    fetch.wait()

    @pl.loop(0, 3)
    def _(f):
        for part in range(2):
            rows = raw[f, part].astype(F32)
            for tx in range(4):
                for t in range(8):
                    at = pl.ds(256 * f + 64 * tx + 8 * t + part, 4, stride=2)
                    mixed[at, :] = rows[4 * tx : 4 * tx + 4, 128 * t : 128 * t + 128]
        for tx in range(4):
            at = pl.ds(pl.multiple_of(256 * f + 64 * tx, 64), 64)
            wsrc[f, tx] = mixed[at, :].astype(BF)

    pl.semaphore_wait(barrier, 11 + 12 - loops + jnp.where(active, 16 - loops, 0))

    @pl.when(gives)
    def _():
        over(0).start()
        over(1).start()
        here.wait()

    @pl.when(takes)
    def _():
        came_over(0).wait()

    @pl.when(active)
    def _():
        for part in range(2):
            for way in range(2):
                ring_copy(way, 0, part).start()

    for step in range(1, 8):
        for copy in y_copies(step):
            copy.start()

    @pl.loop(0, 12)
    def _(i):
        same = is_me(*wave_out(i))

        @pl.when(same)
        def _():
            pltpu.make_async_copy(wsrc.at[i // 4, i % 4], wave.at[a % 16], l_sem.at[1]).start()

        @pl.when(jnp.logical_not(same))
        def _():
            wave_copy(i).start()

    for step in range(1, 8):
        for copy in y_copies(step):
            copy.wait_recv()

    @pl.loop(0, 12)
    def _(i):
        @pl.when(jnp.logical_not(is_me(*wave_out(i))))
        def _():
            for copy in list_copies(i)[:2]:
                copy.start()

    @pl.loop(0, 12)
    def _(i):
        @pl.when(jnp.logical_not(is_me(*wave_out(i))))
        def _():
            list_copies(i)[2].start()

    @pl.when(jnp.logical_and(gives, near))
    def _():
        fac_all[:, slot] = fac_y[...]
        ints_all[:, slot] = ints_y[...]

    def ring_steps(these):
        for way, step, part in these:
            ring_copy(way, step, part).wait_recv()
            if (way, step + 1, part) in ring:
                ring_copy(way, step + 1, part).start()
            cross(way, step, part).start()
            if (way, step, part) in whole:
                share(way, step, part).start()

    def cross_steps(these):
        for copy in these:
            came_across, onward = pass_on(*copy)
            came_across.wait()
            if copy in whole:
                onward.start()

    @pl.when(active)
    def _():
        ring_steps(ring[:4])

        @pl.loop(0, 16)
        def _(i):
            same = is_me(*wave_in(i))

            @pl.when(same)
            def _():
                arrival(wave.at[i], l_sem.at[1]).wait()

            @pl.when(jnp.logical_not(same))
            def _():
                arrival(wave.at[i], w_recv.at[i]).wait()

            at = pl.ds(pl.multiple_of(64 + 64 * i, 64), 64)
            rows = wave[i]
            field[0, at, :128] = rows
            field[0, at, 128:] = turned(rows.astype(F32)).astype(BF)

        edges(0, 0).start()
        edges(1, 0).start()
        prod[pl.ds(8 * DEAD, 8), :] = jnp.zeros((8, 128), F32)
        ring_steps(ring[4:8])
        cross_steps(ring[:4])
        ring_steps(ring[8:12])
        cross_steps(ring[4:8])

        @pl.loop(0, 16)
        def _(i):
            @pl.when(jnp.logical_not(is_me(*wave_in(i))))
            def _():
                at = (i % 4) * 4 + i // 4
                arrival(fac_all.at[pl.ds(0, 2), at], m_recv.at[0, at]).wait()
                arrival(ints_all.at[:, at], m_recv.at[1, at]).wait()

        to_scalars = pltpu.make_async_copy(ints_all, lists, l_sem.at[2])
        to_scalars.start()
        ring_steps(ring[12:])
        cross_steps(ring[8:])
        to_scalars.wait()

        @pl.when(takes)
        def _():
            came_over(1).wait()

        for copy in whole:
            share(*copy).wait_recv()
            pass_on(*copy)[1].wait_recv()

        batches = ((0, 5), (5, 2), (7, 1))

        def image_copy(batch, step):
            first, count = batches[batch]
            to = (x + step) % 4
            return remote(
                img.at[pl.ds(first, count), pl.ds(4 * to, 4)], in_x.at[step, pl.ds(first, count)],
                i_send.at[batch, step], i_recv.at[batch, step], d, z, to, c,
            )

        def owner_copy(level, k):
            return remote(
                x_sum.at[level, k], in_yz.at[d, z], o_send.at[level, k], o_recv.at[d],
                level, 4 * c + k, x, c,
            )

        def is_owner(level, k):
            return jnp.logical_and(level == d, 4 * c + k == z)

        def send_images(batch):
            for step in range(1, 4):
                image_copy(batch, step).start()

        def hand_in(batch):
            for step in range(1, 4):
                image_copy(batch, step).wait_recv()

            @pl.loop(batches[batch][0], sum(batches[batch]))
            def _(level):
                x_sum[level] = (img[level, pl.ds(4 * x, 4)] + in_x[1, level]) + (
                    in_x[2, level] + in_x[3, level]
                )
                for k in range(4):
                    @pl.when(is_owner(level, k))
                    def _():
                        in_yz[d, z] = x_sum[level, k]

                    @pl.when(jnp.logical_not(is_owner(level, k)))
                    def _():
                        owner_copy(level, k).start()

        def group(level, now, g):
            later = 1 - now
            for m in range(16):
                new = []
                for r in (2 * m, 2 * m + 1):
                    block = 4 * g + r // 8
                    at = (block % 4) * 4 + block // 4
                    parts = []
                    for k in range(10):
                        parts.append(prod[pl.ds(lists[level, at, 0, r % 8 * 10 + k], 8), :])
                    while len(parts) > 1:
                        parts = [sum(parts[i + 1 : i + 2], parts[i]) for i in range(0, len(parts), 2)]
                    row = parts[0] * fac_all[level, at, r % 8 : r % 8 + 1, :]
                    img[level, at, r % 8 : r % 8 + 1, :] = jnp.sum(row * row, axis=0, keepdims=True)
                    new.append(row)
                pair = jnp.concatenate(new, 0)
                at = pl.ds(pl.multiple_of(64 + 256 * g + 16 * m, 16), 16)
                field[later, at, :128] = pair.astype(BF)
                field[later, at, 128:] = turned(pair).astype(BF)

        @pl.loop(0, 8)
        def _(level):
            now = level % 2

            @pl.when(level == 2)
            def _():
                @pl.loop(0, 16)
                def _(i):
                    @pl.when(jnp.logical_not(is_me(*wave_in(i))))
                    def _():
                        at = (i % 4) * 4 + i // 4
                        arrival(fac_all.at[pl.ds(2, 6), at], m_recv.at[2, at]).wait()

            for way in range(2):
                edges(way, now).wait()
            for p in range(4):
                b0, b1 = pool_all[level, 2 * p], pool_all[level, 2 * p + 1]
                weights = jnp.concatenate(
                    [
                        jnp.concatenate([b0[:, :128], b1[:, :128]], 1),
                        jnp.concatenate([b0[:, 128:], b1[:, 128:]], 1),
                    ],
                    0,
                )
                product = jnp.dot(field[now], weights, preferred_element_type=F32)
                for k in range(2):
                    rows = pl.ds((2 * p + k) * 8 * WIDE, 8 * WIDE)
                    prod[rows, :] = product[:, 128 * k : 128 * k + 128]

            @pl.loop(0, 2)
            def _(i):
                group(level, now, 3 * i)

            @pl.when(level < 7)
            def _():
                for way in range(2):
                    edges(way, 1 - now).start()

            @pl.loop(1, 3, unroll=True)
            def _(g):
                group(level, now, g)

            for batch in range(3):
                @pl.when(level == sum(batches[batch]) - 1)
                def _():
                    send_images(batch)

        for batch in range(3):
            hand_in(batch)

        for batch in range(3):
            for step in range(1, 4):
                image_copy(batch, step).wait_send()

        @pl.loop(0, 8)
        def _(level):
            for k in range(4):
                @pl.when(jnp.logical_not(is_owner(level, k)))
                def _():
                    owner_copy(level, k).wait_send()

    echo = remote(done, got, e_sem.at[0], e_sem.at[1], d, z, x, other)

    @pl.when(near)
    def _():
        total = jnp.zeros((8, 128), F32)
        for fd in range(8):
            local = jnp.logical_and(active, d == fd)

            @pl.when(local)
            def _():
                arrival(in_yz.at[fd, pl.ds(0, 5)], o_recv.at[fd]).wait()

            @pl.when(jnp.logical_not(local))
            def _():
                arrival(in_yz.at[fd, pl.ds(0, 6)], o_recv.at[fd]).wait()

        for fd in range(8):
            for fz in range(6):
                total = total + in_yz[fd, fz]
        done[...] = total
        echo.start()
        out[...] = total
        echo.wait_send()

    @pl.when(jnp.logical_not(near))
    def _():
        echo.wait_recv()
        out[...] = got[...]

    for step in range(1, 8):
        for copy in y_copies(step):
            copy.wait_send()

    @pl.loop(0, 12)
    def _(i):
        @pl.when(jnp.logical_not(is_me(*wave_out(i))))
        def _():
            wave_copy(i).wait_send()
            for copy in list_copies(i):
                copy.wait_send()

    @pl.when(gives)
    def _():
        over(0).wait_send()
        over(1).wait_send()

    @pl.when(active)
    def _():
        for way, step, part in ring:
            ring_copy(way, step, part).wait_send()
            cross(way, step, part).wait_send()
        for copy in whole:
            share(*copy).wait_send()
            pass_on(*copy)[1].wait_send()


def run(surface, refl, tiles, blocks, counts, pool):
    dma = pltpu.SemaphoreType.DMA
    vmem = pltpu.VMEM
    return pl.pallas_call(
        kernel,
        out_shape=jax.ShapeDtypeStruct((8, 128), F32),
        in_specs=[ANY, VMEM, VMEM, VMEM, pl.BlockSpec(memory_space=pltpu.SMEM), ANY],
        out_specs=VMEM,
        scratch_shapes=[
            vmem((3, 2, 16, 1024), BF),
            vmem((768, 128), F32),
            vmem((3, 4, 64, 128), BF),
            vmem((8, 128), jnp.int32),
            vmem((8, 8, 128), F32),
            vmem((8, 1, 128), jnp.int32),
            vmem((16, 64, 128), BF),
            vmem((2, 8 * WIDE, 256), BF),
            vmem((8, 8, 128, 256), BF),
            vmem((8, 16, 8, 128), F32),
            vmem((8, 16, 1, 128), jnp.int32),
            pltpu.SMEM((8, 16, 1, 128), jnp.int32),
            vmem((8 * DEAD + 8, 128), F32),
            vmem((8, 16, 8, 128), F32),
            vmem((4, 8, 4, 8, 128), F32),
            vmem((8, 4, 8, 128), F32),
            vmem((8, 8, 8, 128), F32),
            vmem((8, 128), F32),
            vmem((8, 128), F32),
            dma((8,)), dma((12,)), dma((16,)), dma((2, 8)), dma((2, 8)), dma((3, 12)), dma((3, 16)),
            dma((2, 8)), dma((2, 8)), dma((2, 8)), dma((2, 8)),
            dma((2, 8)), dma((2, 8)), dma((2, 8)), dma((2, 8)),
            dma((2, 2)), dma((2, 2)), dma((3, 4)), dma((3, 4)), dma((8, 4)), dma((8,)), dma((2,)),
        ],
        compiler_params=pltpu.CompilerParams(
            has_side_effects=True, collective_id=1, vmem_limit_bytes=60 * 2**20
        ),
        name="levels",
    )(surface, refl, tiles, blocks, counts, pool)


def per_device(surface, refl, pool, tile_ids, block_ids, counts):
    image = run(surface, refl.reshape(8, 128), tile_ids[0], block_ids[0], counts, pool)
    return (image / 768.0).reshape(1, 1024)


def solution(mesh):
    placed = (
        P("freq", None, None, "lat"),
        P("depth", "lat"),
        P("depth", "freq", None, None, None),
        P("depth", "lat", None),
        P("depth", "lat", None),
        P("depth", "lat"),
    )
    return jax.shard_map(
        per_device, mesh=mesh, in_specs=placed, out_specs=P("depth", "lat"), check_vma=False
    )
```
